128 devices in a mesh: gz: 4 (over x), xy: 32 (over y, z, core).
Axes of the slice: x: 4, y: 4, z: 4, core: 2. Of those that a mesh axis runs over, the one named last changes fastest.
Arguments:
- em_volume: bfloat16 [32, 8, 128, 128], P('xy', 'gz'), may hold values from -6 to 6
- neighbours: int32 [32, 8], P('xy'), may hold values from -1 to 31, as said below
- first_kernel: bfloat16 [28, 9], replicated, may hold values from -3 to 3
- second_kernel: bfloat16 [28, 28, 27], replicated, may hold values from -0.3125 to 0.3125
- coarse_kernel: bfloat16 [56, 28, 27], replicated, may hold values from -0.3125 to 0.3125
- up_kernel: bfloat16 [28, 56, 4], replicated, may hold values from -1 to 1
- head_kernel: bfloat16 [3, 28], replicated, may hold values from -1.5 to 1.5
Outputs:
- affinity_logits: float32 [32, 3, 8, 128, 128], P('xy', None, 'gz')
The draws below stay inside these ranges and needn't reach their ends.
Inputs may be any that keep to these rules, and one draw needn't show every extreme that they name: `neighbours`: the blocks occupy distinct positions of one grid of 8 columns; row b lists the blocks at the positions north, south, west, east, north-west, north-east, south-west and south-east of block b, north being the lower row and west the lower column, and -1 where that position holds no block or lies outside the grid. The lists are consistent with the one grid.
All inputs are finite; a program needn't handle non-finite values.
Results may differ from the reference program's by a relative error of at most 0.015.
Values may be sent and summed in bfloat16 or wider, within the bound.
No kernel may reach another device: no remote copies, remote signals or barrier semaphores. Data moves between devices by JAX's collectives and lax.ppermute only.
A program may use at most 256 MiB of HBM per device.

```python
import jax
import jax.numpy as jnp
from jax import lax

BS = 128
C0 = 28
C1 = 56
GRID_COLS = 8
NBLK = 32
DZ = 8


def draw_neighbours(key, part):
    key = jax.random.fold_in(key, 11)
    cells = 2 * NBLK
    lines = cells // GRID_COLS
    order = jax.random.permutation(key, cells).astype(jnp.int32)
    place = order[:NBLK]
    occupant = jnp.full((cells,), -1, jnp.int32).at[place].set(jnp.arange(NBLK, dtype=jnp.int32))
    line = place // GRID_COLS
    column = place % GRID_COLS
    gathered = []
    for line_step, column_step in ((-1, 0), (1, 0), (0, -1), (0, 1), (-1, -1), (-1, 1), (1, -1), (1, 1)):
        near_line = line + line_step
        near_column = column + column_step
        inside = (near_line >= 0) & (near_line < lines) & (near_column >= 0) & (near_column < GRID_COLS)
        spot = jnp.clip(near_line, 0, lines - 1) * GRID_COLS + jnp.clip(near_column, 0, GRID_COLS - 1)
        gathered.append(jnp.where(inside, occupant[spot], -1))
    return jnp.stack(gathered, axis=1).astype(jnp.int32)


def shard_levels(rng, dims, split, low, top_value):
    gain, own = 1.0, jax.random.fold_in(rng, 6)
    for position, parts in split:
        draws = jnp.exp(jax.random.uniform(jax.random.fold_in(own, position), (parts,), jnp.float32, low / len(split), top_value / len(split)))
        gain = gain * jnp.repeat(draws, dims[position] // parts).reshape([-1 if axis == position else 1 for axis in range(len(dims))])
    return gain


def scatter_about(rng, shape, spread, limit, cuts=(), held_as=jnp.bfloat16):
    drawn = spread * jax.random.normal(rng, shape, jnp.float32)
    if cuts:
        drawn = drawn * shard_levels(rng, shape, cuts, -0.22, 0.18)
    return jnp.clip(drawn, -limit, limit).astype(held_as)


def setup_inputs(seed: int = 0) -> dict:
    key_list = jax.random.split(jax.random.key(seed), 8)
    em_volume = scatter_about(key_list[0], (NBLK, DZ, BS, BS), 1.0, 6.0, ((0, 32), (1, 4)))
    neighbours = draw_neighbours(jax.random.fold_in(key_list[7], 71), 0)
    first_kernel = scatter_about(key_list[2], (C0, 9), 4 ** -0.5, 3.0)
    second_kernel = scatter_about(key_list[3], (C0, C0, 27), (27 * C0 // 2) ** -0.5, 0.3125)
    coarse_kernel = scatter_about(key_list[4], (C1, C0, 27), (27 * C0 // 2) ** -0.5, 0.3125)
    up_kernel = scatter_about(key_list[5], (C0, C1, 4), (C1 // 2) ** -0.5, 1.0)
    head_kernel = scatter_about(key_list[6], (3, C0), (C0 // 2) ** -0.5, 1.5)
    return dict(em_volume=em_volume, neighbours=neighbours, first_kernel=first_kernel, second_kernel=second_kernel, coarse_kernel=coarse_kernel, up_kernel=up_kernel, head_kernel=head_kernel)


def fetch(source, neighbours, direction):
    index = neighbours[:, direction]
    values = jnp.take(source, jnp.maximum(index, 0), axis=0)
    keep = (index >= 0).reshape((-1,) + (1,) * (source.ndim - 1))
    return jnp.where(keep, values, jnp.zeros_like(values))


def cycle(features, neighbours):
    top = features[:, :, :, :1, :]
    bottom = features[:, :, :, -1:, :]
    left = features[:, :, :, :, :1]
    right = features[:, :, :, :, -1:]
    north = fetch(bottom, neighbours, 0)
    south = fetch(top, neighbours, 1)
    west = fetch(right, neighbours, 2)
    east = fetch(left, neighbours, 3)
    north_west = fetch(bottom[..., -1:], neighbours, 4)
    north_east = fetch(bottom[..., :1], neighbours, 5)
    south_west = fetch(top[..., -1:], neighbours, 6)
    south_east = fetch(top[..., :1], neighbours, 7)
    upper = jnp.concatenate([north_west, north, north_east], axis=4)
    middle = jnp.concatenate([west, features, east], axis=4)
    lower = jnp.concatenate([south_west, south, south_east], axis=4)
    return jnp.concatenate([upper, middle, lower], axis=3)


def deepen(features):
    return jnp.pad(features, ((0, 0), (0, 0), (1, 1), (0, 0), (0, 0)))


def convolve(extended, kernel, depth):
    outputs, inputs = kernel.shape[0], kernel.shape[1]
    filters = kernel.astype(jnp.float32).reshape(outputs, inputs, depth, 3, 3)

    def single(block):
        return lax.conv_general_dilated(block.astype(jnp.float32)[None], filters, (1, 1, 1), "VALID",
                                        dimension_numbers=("NCDHW", "OIDHW", "NCDHW"),
                                        precision=lax.Precision.HIGHEST)[0]

    return lax.map(single, extended)


def pool(skip):
    blocks, channels, planes, height, width = skip.shape

    def single(block):
        grid = block.astype(jnp.float32).reshape(channels, planes, height // 2, 2, width // 2, 2)
        return (jnp.sum(grid, axis=(3, 5)) * 0.25).astype(jnp.bfloat16)

    return lax.map(single, skip)


def reference(em_volume, neighbours, first_kernel, second_kernel, coarse_kernel, up_kernel, head_kernel):
    raw = em_volume[:, None]
    first_taps = first_kernel.reshape(first_kernel.shape[0], 1, 9)
    first = jax.nn.relu(convolve(cycle(raw, neighbours), first_taps, 1)).astype(jnp.bfloat16)
    skip = jax.nn.relu(convolve(deepen(cycle(first, neighbours)), second_kernel, 3)).astype(jnp.bfloat16)
    pooled = pool(skip)
    coarse = jax.nn.relu(convolve(deepen(cycle(pooled, neighbours)), coarse_kernel, 3)).astype(jnp.bfloat16)
    up_float = up_kernel.astype(jnp.float32)
    head_float = head_kernel.astype(jnp.float32)

    def finish(pair):
        coarse_block, skip_block = pair
        channels, planes, height, width = coarse_block.shape
        upward = jnp.einsum("ock,czyx->ozyxk", up_float, coarse_block.astype(jnp.float32),
                            precision=lax.Precision.HIGHEST)
        upward = upward.reshape(-1, planes, height, width, 2, 2)
        upward = upward.transpose(0, 1, 2, 4, 3, 5).reshape(-1, planes, 2 * height, 2 * width)
        joined = jax.nn.relu(upward + skip_block.astype(jnp.float32)).astype(jnp.bfloat16)
        return jnp.einsum("kc,czyx->kzyx", head_float, joined.astype(jnp.float32),
                          precision=lax.Precision.HIGHEST)

    return lax.map(finish, (coarse, skip))
```

```python
import jax
import jax.numpy as jnp
from jax import lax
from jax.experimental import pallas as pl
from jax.experimental.pallas import tpu as pltpu
from jax.sharding import PartitionSpec as P

F32 = jnp.float32
BF16 = jnp.bfloat16
PITCH = 40
LINES = 66
FIRST_OFF = 256.0
SKIP_OFF = 65536.0
VMEM = pl.BlockSpec(memory_space=pltpu.VMEM)
SMEM = pl.BlockSpec(memory_space=pltpu.SMEM)
NT = (((1,), (1,)), ((), ()))


def iota(shape, dim):
    return lax.broadcasted_iota(jnp.int32, shape, dim)


def dot(a, b):
    return jnp.dot(a, b, preferred_element_type=F32)


def dot_nt(a, b):
    return lax.dot_general(a, b, NT, preferred_element_type=F32)


def pack_kernel(nb, prev, own, nxt, slots, rows):
    slots[...] = jnp.zeros(slots.shape, BF16)
    rows[...] = jnp.zeros(rows.shape, F32)
    lane, line = iota((16, 128), 1), iota((16, 128), 0)
    edge = jnp.where(lane == jnp.where(line < 4, line, 120 + line), 1.0, 0.0).astype(BF16)
    for z in range(6):
        plane = (prev, own, nxt)[z // 2][z % 2]
        rows[0, pl.ds(z, 4, stride=8), :] = plane[0:16].astype(F32)[0:4]
        rows[1, pl.ds(z, 4, stride=8), :] = plane[112:128].astype(F32)[12:16]
        sides = dot_nt(edge, plane)
        rows[2, pl.ds(z, 4, stride=8), :] = sides[0:4]
        rows[3, pl.ds(z, 4, stride=8), :] = sides[4:8]
    for k, strip in enumerate((0, 1, 2, 3, 0, 0, 1, 1)):

        @pl.when(nb[0, k] >= 0)
        def _():
            slots[jnp.maximum(nb[0, k], 0)] = rows[strip].astype(BF16)


def weights_kernel(first, second, coarse, up, head, wf, ws, wc, wu, ht, taps2, tapsc, taps1, tapsh):
    lane = iota((32, 128), 1)
    turned = jnp.concatenate([second[...].astype(F32)] * 4, axis=0).T
    taps1[...] = turned
    for tap in range(27):
        fill = jnp.where((iota((4, 128), 0) == 0) & (iota((4, 128), 1) % 32 < 28), -SKIP_OFF, 0.0)
        taps2[tap * 32 : tap * 32 + 28, :] = taps1[pl.ds(tap, 28, stride=27), :]
        taps2[tap * 32 + 28 : tap * 32 + 32, :] = fill if tap == 13 else jnp.zeros((4, 128), F32)
    for z in range(4):
        for row in range(4):
            for col in range(4):
                block = (z * 2 + row // 2) * 8 + (col // 2) * 4 + (row % 2) * 2 + col % 2
                for half in range(2):
                    value = jnp.zeros((32, 128), F32)
                    for slot in range(4):
                        dz, dr, dc = z - half, row - slot // 2, col - slot % 2
                        if 0 <= dz < 3 and 0 <= dr < 3 and 0 <= dc < 3:
                            tap = dz * 9 + dr * 3 + dc
                            value = jnp.where(lane // 32 == slot, taps2[tap * 32 : tap * 32 + 32, :], value)
                    ws[block * 32 : block * 32 + 32, half * 128 : half * 128 + 128] = value.astype(BF16)
    taps1[...] = jnp.concatenate([coarse[...].astype(F32)] * 2, axis=0).T
    for tap in range(27):
        tapsc[tap * 32 : tap * 32 + 28, :] = taps1[pl.ds(tap, 28, stride=27), :]
        tapsc[tap * 32 + 28 : tap * 32 + 32, :] = jnp.zeros((4, 128), F32)
    for dy in range(3):
        for z in range(4):
            for col in range(4):
                block = (dy * 4 + z) * 4 + col
                for half in range(2):
                    value = jnp.zeros((32, 128), F32)
                    for slot in range(2):
                        dz, dc = z - slot, col - half
                        if 0 <= dz < 3 and 0 <= dc < 3:
                            tap = dz * 9 + dy * 3 + dc
                            value = jnp.where(lane // 64 == slot, tapsc[tap * 32 : tap * 32 + 32, :], value)
                    wc[block * 32 : block * 32 + 32, half * 128 : half * 128 + 128] = value.astype(BF16)
    taps1[0:256, :] = jnp.concatenate([up[...].astype(F32)] * 4, axis=0).T
    mixed = jnp.zeros((64, 128), F32)
    for tap in range(4):
        mixed = jnp.where(iota((64, 128), 1) // 32 == tap, taps1[pl.ds(tap, 64, stride=4), :], mixed)
    mixed = jnp.where(iota((64, 128), 0) < 56, mixed, 0.0).astype(BF16)
    nothing = jnp.zeros((64, 128), BF16)
    wu[0:64, 0:128] = mixed
    wu[0:64, 128:256] = nothing
    wu[64:128, 0:128] = nothing
    wu[64:128, 128:256] = mixed
    tapsh[...] = jnp.zeros(tapsh.shape, F32)
    tapsh[0:28, 0:9] = first[...].astype(F32)
    by_tap = jnp.concatenate([tapsh[0:32, :]] * 4, axis=0).T
    by_tap = jnp.concatenate([by_tap] * 3, axis=1)
    at, to = iota((256, 384), 0), iota((256, 384), 1)
    row = (at // 128) * 2 + (at // 8) % 2 - (to // 64) % 2
    col = (at // 16) % 8 - (to // 128) * 2 - (to // 32) % 2
    window = jnp.where((row >= 0) & (row < 3) & (col >= 0) & (col < 3), row * 3 + col, -1)
    spread = jnp.zeros((256, 384), F32)
    for tap in range(9):
        spread = jnp.where(window == tap, by_tap[tap : tap + 1, :], spread)
    off = jnp.where(to % 32 < 28, -FIRST_OFF, jnp.where(to % 32 == 28, 1.0, 0.0))
    off = jnp.where((window == 4) & (at % 8 == 6), off, 0.0)
    for z in range(6):
        wf[:, z * 384 : z * 384 + 384] = jnp.where(at % 8 == z, spread, off).astype(BF16)
    tapsh[...] = jnp.zeros(tapsh.shape, F32)
    tapsh[0:3, 0:28] = head[...].astype(F32)
    narrow = tapsh[0:8, :]
    wide = narrow
    for turn in (32, 64, 96):
        wide = wide + pltpu.roll(narrow, turn, 1)
    wide = jnp.concatenate([wide, wide], axis=1)
    at, to = iota((32, 256), 0), iota((32, 256), 1)
    fits = (at // 16 == (to // 32) % 2) & (at % 2 == (to // 64) % 2) & ((at // 2) % 2 == to // 128)
    value = jnp.zeros((32, 256), F32)
    for k in range(3):
        value = jnp.where(fits & ((at % 16) // 4 == k), wide[k : k + 1, :], value)
    ht[...] = value.astype(BF16)


def main_kernel(meta, prev, own, nxt, recv, wf, ws, wc, wu, ht, out, ext, strips, turned, shifted, taps, first, pooled, skip, flat, mixed):
    ext[...] = jnp.zeros(ext.shape, F32)
    side_lane = iota((32, 128), 1)
    plane_row = iota((32, 128), 0) % 8
    gone = jnp.where(plane_row == 6, 1.0, 0.0)

    def strip(k):
        have = meta[0, k] >= 0
        return jnp.where(have, recv[jnp.maximum(meta[0, k], 0)].astype(F32), gone)

    north, south, west, east = strip(0), strip(1), strip(2), strip(3)
    for start, middle, left, right in ((0, north, strip(4), strip(5)), (1056, south, strip(6), strip(7))):
        ext[0, start : start + 32, :] = middle
        ext[1, start : start + 32, :] = jnp.where(side_lane < 4, right, jnp.where(side_lane >= 124, left, 0.0))
    strips[0] = west
    strips[1] = east
    turned[...] = jnp.zeros(turned.shape, F32)
    for z in range(7):
        if z < 6:
            plane = (prev, own, nxt)[z // 2][z % 2]
            ext[0, pl.ds(32 + z, 128, stride=8), :] = plane.astype(F32)
        turned[0:4, :] = strips[1, pl.ds(z, 4, stride=8), :]
        turned[124:128, :] = strips[0, pl.ds(z, 4, stride=8), :]
        ext[1, pl.ds(32 + z, 128, stride=8), :] = turned[...].T

    for c in range(8):
        for part in range(4):
            rows = pl.ds(part * 272, 272)
            value = jnp.concatenate([ext[0, rows, :], ext[1, rows, :]], axis=1)
            if c != 4:
                value = pltpu.roll(value, (4 - c) % 256, 1)
            shifted[c, rows, :] = value.astype(BF16)

    pick = jnp.where((iota((PITCH, 256), 1) == 4 * iota((PITCH, 256), 0)) & (iota((PITCH, 256), 0) < 33), 1.0, 0.0)
    pick = pick.astype(BF16)

    def gather(t, _):
        lines = [
            shifted[c, pl.ds(pl.multiple_of(t * 32, 32) + 16 * h, 16), :] for h in range(2) for c in range(8)
        ]
        got = dot_nt(pick, jnp.concatenate(lines, axis=0))
        both = jnp.concatenate([got[:, 0:128], got[:, 128:256]], axis=0)
        taps[pl.ds(pl.multiple_of(t * 2 * PITCH, 2 * PITCH), 2 * PITCH), :] = both.astype(BF16)
        return 0

    lax.fori_loop(0, 34, gather, 0)

    def first_rows(base, count):
        below = taps[pl.ds(base + 32, count + 16), :][8 : count + 8]
        window = jnp.concatenate([taps[pl.ds(base, count), :], below], axis=1)
        for z in range(0, 6, 2):
            got = jnp.maximum(dot(window, wf[:, z * 384 : z * 384 + 768]), 0.0).astype(BF16)
            first[z, pl.ds(base, count), :] = got[:, 0:384]
            first[z + 1, pl.ds(base, count), :] = got[:, 384:768]

    def first_step(g, _):
        first_rows(pl.multiple_of(g * 240, 240), 240)
        return 0

    lax.fori_loop(0, 11, first_step, 0)
    first_rows(2640, 48)

    at, to = iota((256, 256), 0), iota((256, 256), 1)
    meets = (at // 128 == to // 128) & (at % 32 == to % 32)
    outside = ((meta[0, 8] == 0, False), (False, meta[0, 8] == 3))
    pools = []
    for p in range(2):
        scale = jnp.where(to < 128, jnp.where(outside[p][0], 0.0, 0.25), jnp.where(outside[p][1], 0.0, 0.25))
        pools.append([jnp.where(meets & ((to // 32) % 2 == par), scale, 0.0).astype(BF16) for par in range(2)])

    def skip_step(g, _):
        base = pl.multiple_of(g * 240, 240)
        lines = [
            (first[z, pl.ds(base, 240), :], first[z, pl.ds(base + 32, 256), :][8:248]) for z in range(6)
        ]
        for p in range(2):
            mean = None
            for par in range(2):
                total = None
                for z in range(4):
                    for dy in range(2):
                        window = lines[2 * p + z][dy][:, par * 128 : par * 128 + 256]
                        at = (z * 2 + dy) * 256
                        term = dot(window, ws[at : at + 256, :])
                        total = term if total is None else total + term
                total = jnp.maximum(total, 0.0)
                term = dot(total.astype(BF16), pools[p][par])
                mean = term if mean is None else mean + term
                inner = total[:, 128:256] if p == 0 else total[:, 0:128]
                if par == 0:
                    inner = pltpu.roll(inner, 239, 0)
                for y in range(6):
                    rows = pl.ds(pl.multiple_of(g * 192, 192) + y * 32, 32)
                    skip[1 - par, rows, p * 128 : p * 128 + 128] = inner[y * PITCH : y * PITCH + 32].astype(BF16)
            after = pltpu.roll(mean, 239, 0)
            mean = jnp.where(iota((240, 256), 1) % 128 < 64, mean, after)
            for y in range(6):
                rows = pl.ds(pl.multiple_of(g * 192, 192) + y * 32, 32)
                pooled[p, rows, :] = mean[y * PITCH : y * PITCH + 32].astype(BF16)
        return 0

    lax.fori_loop(0, 11, skip_step, 0)

    def last_step(g, _):
        base = pl.multiple_of(g * 256, 256)
        total = None
        for dy in range(3):
            for p in range(2):
                at = (dy * 2 + p) * 256
                term = dot(pooled[p, pl.ds(base + dy * 32, 256), :], wc[at : at + 256, :])
                total = term if total is None else total + term
        coarse = jnp.maximum(total, 0.0).astype(BF16)
        joined = []
        for side in range(2):
            upward = dot(coarse[:, side * 128 : side * 128 + 128], wu[...])
            upward = upward + skip[side, pl.ds(base + 32, 256), :].astype(F32)
            joined.append(jnp.maximum(upward, 0.0).astype(BF16))
        for half in range(2):
            lines = [joined[side][y * 32 : y * 32 + 32] for y in range(half * 4, half * 4 + 4) for side in range(2)]
            logits = dot_nt(ht[...], jnp.concatenate(lines, axis=0))
            high = logits.astype(BF16)
            low = (logits - high.astype(F32)).astype(BF16)
            for pair in range(2):
                rows = pl.ds(pl.multiple_of(g * 64, 64) + (half * 2 + pair) * 16, 16)
                lanes = slice(pair * 128, pair * 128 + 128)
                flat[rows, 0:128] = high[0:16, lanes]
                flat[rows, 128:256] = low[0:16, lanes]
                flat[rows, 256:384] = high[16:32, lanes]
                flat[rows, 384:512] = low[16:32, lanes]
        return 0

    lax.fori_loop(0, 8, last_step, 0)

    at, to = iota((512, 256), 0), iota((512, 256), 1)
    column = 4 * (at % 32) + 2 * ((at // 32) % 2) + at // 256
    place = jnp.where(((at // 64) % 2 == to // 128) & (column == to % 128), 1.0, 0.0).astype(BF16)
    logits = dot(flat[...], place)
    mixed[0] = logits[:, 0:128]
    mixed[1] = logits[:, 128:256]
    for k in range(3):
        for z in range(2):
            for line in range(4):
                row = k * 4 + z * 2 + line % 2
                out[0, k, z, pl.ds(line, 32, stride=4), :] = mixed[line // 2, pl.ds(row, 32, stride=16), :]


def on_device(em_volume, neighbours, first_kernel, second_kernel, coarse_kernel, up_kernel, head_kernel):
    own = em_volume[0]
    steps = lax.axis_size("gz")
    prev = lax.ppermute(own, "gz", [(i, i + 1) for i in range(steps - 1)])
    nxt = lax.ppermute(own, "gz", [(i + 1, i) for i in range(steps - 1)])
    limit = pltpu.CompilerParams(vmem_limit_bytes=56 * 2**20)

    second = jnp.pad(second_kernel.reshape(28, 756), ((0, 4), (0, 12)))
    coarse = jnp.pad(coarse_kernel.reshape(56, 756), ((0, 8), (0, 12)))
    up = jnp.pad(up_kernel.reshape(28, 224), ((0, 4), (0, 32)))
    shapes = [(256, 2304), (2048, 256), (1536, 256), (128, 256), (32, 256)]
    weights = pl.pallas_call(
        weights_kernel,
        out_shape=[jax.ShapeDtypeStruct(s, BF16) for s in shapes],
        in_specs=[VMEM] * 5,
        out_specs=[VMEM] * 5,
        scratch_shapes=[
            pltpu.VMEM((864, 128), F32),
            pltpu.VMEM((864, 128), F32),
            pltpu.VMEM((768, 128), F32),
            pltpu.VMEM((32, 128), F32),
        ],
        compiler_params=limit,
        cost_estimate=pl.CostEstimate(flops=10**8, bytes_accessed=4 * 10**6, transcendentals=0),
        name="weights",
    )(first_kernel, second, coarse, up, head_kernel)

    slots = pl.pallas_call(
        pack_kernel,
        out_shape=jax.ShapeDtypeStruct((32, 32, 128), BF16),
        in_specs=[SMEM] + [VMEM] * 3,
        out_specs=VMEM,
        scratch_shapes=[pltpu.VMEM((4, 32, 128), F32)],
        compiler_params=limit,
        name="pack",
    )(neighbours, prev, own, nxt)
    recv = lax.all_to_all(slots, "xy", 0, 0, tiled=True)

    place = jnp.full((1, 1), lax.axis_index("gz"), jnp.int32)
    meta = jnp.concatenate([neighbours, place], axis=1)
    return pl.pallas_call(
        main_kernel,
        out_shape=jax.ShapeDtypeStruct((1, 3, 2, 128, 128), F32),
        in_specs=[SMEM] + [VMEM] * 9,
        out_specs=VMEM,
        scratch_shapes=[
            pltpu.VMEM((2, 1088, 128), F32),
            pltpu.VMEM((2, 32, 128), F32),
            pltpu.VMEM((128, 128), F32),
            pltpu.VMEM((8, 1088, 256), BF16),
            pltpu.VMEM((2736, 128), BF16),
            pltpu.VMEM((6, 2688, 384), BF16),
            pltpu.VMEM((2, LINES * 32, 256), BF16),
            pltpu.VMEM((2, LINES * 32, 256), BF16),
            pltpu.VMEM((512, 512), BF16),
            pltpu.VMEM((2, 512, 128), F32),
        ],
        compiler_params=limit,
        name="layers",
    )(meta, prev, own, nxt, recv, *weights)


def solution(mesh):
    placed = (P("xy", "gz", None, None), P("xy", None), P(), P(), P(), P(), P())
    return jax.shard_map(
        on_device,
        mesh=mesh,
        in_specs=placed,
        out_specs=P("xy", None, "gz", None, None),
        check_vma=False,
    )
```

```python
import jax
import jax.numpy as jnp
from jax import lax
from jax.experimental import pallas as pl
from jax.experimental.pallas import tpu as pltpu
from jax.sharding import PartitionSpec as P

F32 = jnp.float32
BF16 = jnp.bfloat16
LINES = 66
FIRST_LINES, SKIP_LINES, LAST_LINES = 22, 22, 32
FIRST_OFF = 256.0
SKIP_OFF = 65536.0
VMEM = pl.BlockSpec(memory_space=pltpu.VMEM)
SMEM = pl.BlockSpec(memory_space=pltpu.SMEM)
NT = (((1,), (1,)), ((), ()))


def iota(shape, dim):
    return lax.broadcasted_iota(jnp.int32, shape, dim)


def dot(a, b):
    return jnp.dot(a, b, preferred_element_type=F32)


def dot_nt(a, b):
    return lax.dot_general(a, b, NT, preferred_element_type=F32)


def pack_kernel(nb, prev, own, nxt, slots, rows):
    slots[...] = jnp.zeros(slots.shape, BF16)
    lane, line = iota((16, 128), 1), iota((16, 128), 0)
    edge = jnp.where((lane == jnp.where(line < 4, line, 120 + line)) & (line < 8), 1.0, 0.0).astype(BF16)
    planes = jnp.concatenate([ref[z] for ref in (prev, own, nxt) for z in range(2)], axis=0)
    sides = dot_nt(edge, planes)
    for z in range(6):
        at = slice(4 * z, 4 * z + 4)
        rows[0, at, :] = planes[z * 128 : z * 128 + 16].astype(F32)[0:4]
        rows[1, at, :] = planes[z * 128 + 112 : z * 128 + 128].astype(F32)[12:16]
        rows[2, at, :] = sides[0:4, z * 128 : z * 128 + 128]
        rows[3, at, :] = sides[4:8, z * 128 : z * 128 + 128]
    for k, strip in enumerate((0, 1, 2, 3, 2, 3, 2, 3)):

        @pl.when(nb[0, k] >= 0)
        def _():
            slots[jnp.maximum(nb[0, k], 0)] = rows[strip].astype(BF16)


def weights_kernel(first, second, coarse, up, head, wf, ws, wc, wu, wh, taps2, tapsc, part, ups):
    lane = iota((32, 128), 1)
    part[...] = jnp.zeros(part.shape, F32)
    for four in range(7):
        value = jnp.zeros((32, 128), F32)
        for tap in range(4 * four, min(4 * four + 4, 27)):
            part[0:28, 0:28] = second[tap].astype(F32)
            turn = (tap % 4) * 32
            value = value + (pltpu.roll(part[0:32, :], turn, 1) if turn else part[0:32, :])
        turned = jnp.concatenate([value] * 4, axis=0).T
        taps2[four * 128 : four * 128 + 128, :] = turned
    fill = jnp.where(iota((1, 128), 1) % 32 < 28, -SKIP_OFF, 0.0)
    taps2[13 * 32 + 28 : 13 * 32 + 29, :] = fill
    for z in range(4):
        for row in range(4):
            for col in range(4):
                block = (z * 2 + row // 2) * 8 + (col // 2) * 4 + (row % 2) * 2 + col % 2
                for half in range(2):
                    value = jnp.zeros((32, 128), F32)
                    for slot in range(4):
                        dz, dr, dc = z - half, row - slot // 2, col - slot % 2
                        if 0 <= dz < 3 and 0 <= dr < 3 and 0 <= dc < 3:
                            tap = dz * 9 + dr * 3 + dc
                            value = jnp.where(lane // 32 == slot, taps2[tap * 32 : tap * 32 + 32, :], value)
                    ws[block * 32 : block * 32 + 32, half * 128 : half * 128 + 128] = value.astype(BF16)
    part[...] = jnp.zeros(part.shape, F32)
    for tap in range(27):
        part[0:28, 0:56] = coarse[tap].astype(F32)
        tapsc[tap * 32 : tap * 32 + 32, :] = part[0:32, :] + pltpu.roll(part[0:32, :], 64, 1)
    for dy in range(3):
        for z in range(4):
            for col in range(4):
                block = (dy * 4 + z) * 4 + col
                for half in range(2):
                    value = jnp.zeros((32, 128), F32)
                    for slot in range(2):
                        dz, dc = z - slot, col - half
                        if 0 <= dz < 3 and 0 <= dc < 3:
                            tap = dz * 9 + dy * 3 + dc
                            value = jnp.where(lane // 64 == slot, tapsc[tap * 32 : tap * 32 + 32, :], value)
                    wc[block * 32 : block * 32 + 32, half * 128 : half * 128 + 128] = value.astype(BF16)
    part[...] = jnp.zeros(part.shape, F32)
    ups[...] = jnp.zeros(ups.shape, F32)
    ups[:, 0:4, 0:56] = up[...].astype(F32)
    for channel in range(28):
        part[pl.ds(channel, 4, stride=32), :] = ups[channel, 0:4, :]
    mixed = part[...].T[0:64].astype(BF16)
    nothing = jnp.zeros((64, 128), BF16)
    wu[0:64, 0:128] = mixed
    wu[0:64, 128:256] = nothing
    wu[64:128, 0:128] = nothing
    wu[64:128, 128:256] = mixed
    part[...] = jnp.zeros(part.shape, F32)
    part[0:9, 0:28] = first[...].astype(F32)
    by_tap = part[0:16, :]
    by_tap = by_tap + pltpu.roll(by_tap, 32, 1)
    by_tap = by_tap + pltpu.roll(by_tap, 64, 1)
    by_tap = jnp.concatenate([by_tap] * 3, axis=1)
    at, to = iota((256, 384), 0), iota((256, 384), 1)
    row = (at // 128) * 2 + at % 2 - (to // 64) % 2
    col = (at // 2) % 8 - (to // 128) * 2 - (to // 32) % 2
    plane = (at // 16) % 8
    window = jnp.where((row >= 0) & (row < 3) & (col >= 0) & (col < 3), row * 3 + col, -1)
    spread = jnp.zeros((256, 384), F32)
    for tap in range(9):
        spread = jnp.where(window == tap, by_tap[tap : tap + 1, :], spread)
    off = jnp.where(to % 32 < 28, -FIRST_OFF, jnp.where(to % 32 == 28, 1.0, 0.0))
    off = jnp.where((window == 4) & (plane == 6), off, 0.0)
    for z in range(6):
        wf[:, z * 384 : z * 384 + 384] = jnp.where(plane == z, spread, off).astype(BF16)
    part[...] = jnp.zeros(part.shape, F32)
    part[0:3, 0:28] = head[...].astype(F32)
    by_map = part[...].T
    by_map = jnp.concatenate([by_map[0:32]] * 8, axis=0)
    at, to = iota((256, 128), 0), iota((256, 128), 1)
    fits = ((to // 16) % 2 == (at // 32) % 2) & (to % 2 == (at // 64) % 2) & ((to // 2) % 2 == at // 128)
    value = jnp.zeros((256, 128), F32)
    for k in range(3):
        value = jnp.where(fits & ((to % 16) // 4 == k), by_map[:, k : k + 1], value)
    for block in range(4):
        wh[block * 256 : block * 256 + 256, :] = jnp.where(to // 32 == block, value, 0.0).astype(BF16)


def main_kernel(meta, prev, own, nxt, recv, wf, ws, wc, wu, wh, out, ext, strips, turned, taps, edge_taps, first, edge_mean, pooled, skip, high, low, mixed):
    strips[...] = jnp.zeros(strips.shape, F32)
    for k in range(8):
        have = meta[0, k] >= 0
        strips[k, 4:28, :] = jnp.where(have, recv[jnp.maximum(meta[0, k], 0)].astype(F32), 0.0)
        strips[k, 28:32, :] = jnp.full((4, 128), jnp.where(have, 0.0, 1.0), F32)

    ext[...] = jnp.zeros(ext.shape, F32)
    for z in range(7):
        if z < 6:
            ext[z, 4:132, :] = (prev, own, nxt)[z // 2][z % 2].astype(F32)
        ext[z, 0:4, :] = strips[0, 4 * z + 4 : 4 * z + 8, :]
        ext[z, 132:136, :] = strips[1, 4 * z + 4 : 4 * z + 8, :]

    lane = iota((8, 128), 1)
    edge_taps[...] = jnp.zeros(edge_taps.shape, F32)
    for b in range(9):
        lines = [ext[z, 16 * b : 16 * b + 16, :] for z in range(8)]
        turned[b, 8:136, :] = jnp.concatenate(lines, axis=0).T
        for start, sides, shift in ((0, (4, 2, 6), 0), (136, (5, 3, 7), 4)):
            value = jnp.zeros((8, 128), F32)
            for z in range(7):
                rows = slice(4 * z + shift, 4 * z + shift + 8)
                line = strips[sides[1], rows, :]
                if b == 0:
                    line = jnp.where(lane >= 124, strips[sides[0], rows, :], line)
                if b == 8:
                    line = jnp.where(lane < 4, strips[sides[2], rows, :], jnp.where(lane >= 124, line, 0.0))
                turn = (16 * z - 16 * b + 4) % 128
                value = jnp.where(lane // 16 == z, pltpu.roll(line, turn, 1) if turn else line, value)
            turned[b, start : start + 8, :] = value
        parts = [
            jnp.concatenate(
                [turned[b, pl.ds(6 + c, 32, stride=4), :], turned[b, pl.ds(2 + c, 2, stride=132), :]], axis=0
            )
            for c in range(8)
        ]
        for bit in (1, 2, 4):
            side = (iota((34, 128), 1) // (2 * bit)) % 2 == 0
            for a in range(8):
                if not a & bit:
                    one, two = parts[a], parts[a + bit]
                    parts[a] = jnp.where(side, one, pltpu.roll(two, 2 * bit, 1))
                    parts[a + bit] = jnp.where(side, pltpu.roll(one, 128 - 2 * bit, 1), two)
        for y in range(8):
            at = 8 * b + y
            if at < 68:
                taps[at * 32 : at * 32 + 32, :] = parts[y][0:32].astype(BF16)
                edge_taps[0, at : at + 1, :] = parts[y][32:33]
                edge_taps[1, at : at + 1, :] = parts[y][33:34]

    at, to = iota((256, 256), 0), iota((256, 256), 1)
    meets = (at // 128 == to // 128) & (at % 32 == to % 32)
    outside = ((meta[0, 8] == 0, False), (False, meta[0, 8] == 3))
    pools = []
    for p in range(2):
        scale = jnp.where(to < 128, jnp.where(outside[p][0], 0.0, 0.25), jnp.where(outside[p][1], 0.0, 0.25))
        pools.append([jnp.where(meets & ((to // 32) % 2 != par), scale, 0.0).astype(BF16) for par in range(2)])

    def add_dots(pairs):
        total = None
        for a, b in pairs:
            term = dot(a, b)
            total = term if total is None else total + term
        return total

    windows = []
    for side in range(2):
        lines = [edge_taps[side, pl.ds(dy, 80), :].astype(BF16) for dy in range(3)]
        windows += [jnp.concatenate(lines[dy : dy + 2], axis=1) for dy in range(2)]
    edges = jnp.maximum(dot(jnp.concatenate(windows, axis=0), wf[...]), 0.0).astype(BF16)
    for p in range(2):
        pairs = []
        for z in range(4):
            for dy in range(2):
                lanes = (2 * p + z) * 384
                west = edges[dy * 80 : dy * 80 + 80, lanes + 128 : lanes + 384]
                east = edges[160 + dy * 80 : 240 + dy * 80, lanes : lanes + 256]
                pairs.append((jnp.concatenate([west, east], axis=0), ws[(z * 2 + dy) * 256 : (z * 2 + dy) * 256 + 256, :]))
        value = jnp.maximum(add_dots(pairs), 0.0).astype(BF16)
        edge_mean[p, 0] = dot(value[0:80], pools[p][1])
        edge_mean[p, 1] = dot(value[80:160], pools[p][0])

    def first_rows(base, count):
        window = jnp.concatenate([taps[pl.ds(base, count), :], taps[pl.ds(base + 32, count), :]], axis=1)
        for n in range(0, 2304, 256):
            first[pl.ds(base, count), n : n + 256] = jnp.maximum(dot(window, wf[:, n : n + 256]), 0.0).astype(BF16)

    def first_step(g, _):
        first_rows(pl.multiple_of(g * (FIRST_LINES * 32), FIRST_LINES * 32), FIRST_LINES * 32)
        return 0

    lax.fori_loop(0, 66 // FIRST_LINES, first_step, 0)
    first_rows(2112, 32)

    def skip_step(g, _):
        count = SKIP_LINES * 32
        base = pl.multiple_of(g * count, count)
        group = (iota((count, 256), 1) // 32) % 4
        line_row, line_group = iota((32, 256), 0), (iota((32, 256), 1) // 32) % 4
        for p in range(2):
            values = []
            for par in range(2):
                pairs = []
                for z in range(4):
                    for dy in range(2):
                        lanes = (2 * p + z) * 384 + par * 128
                        at = (z * 2 + dy) * 256
                        pairs.append((first[pl.ds(base + dy * 32, count), lanes : lanes + 256], ws[at : at + 256, :]))
                value = jnp.maximum(add_dots(pairs), 0.0).astype(BF16)
                skip[par, pl.ds(base, count), p * 128 : p * 128 + 128] = value[:, 128 - p * 128 : 256 - p * 128]
                values.append(value)
            mean = add_dots([(values[0], pools[p][0]), (values[1], pools[p][1])])
            before, after = pltpu.roll(mean, 1, 0), pltpu.roll(mean, count - 1, 0)
            mean = jnp.where(group == 0, before, jnp.where(group == 3, after, mean))
            for y in range(SKIP_LINES):
                line = mean[y * 32 : y * 32 + 32]
                west = edge_mean[p, 0, pl.ds(g * SKIP_LINES + y, 1), :]
                east = edge_mean[p, 1, pl.ds(g * SKIP_LINES + y, 1), :]
                line = jnp.where((line_row == 0) & (line_group == 0), west, line)
                line = jnp.where((line_row == 31) & (line_group == 3), east, line)
                pooled[p, pl.ds(base + y * 32, 32), :] = line.astype(BF16)
        return 0

    lax.fori_loop(0, 66 // SKIP_LINES, skip_step, 0)

    def last_step(g, _):
        count = LAST_LINES * 32
        base = pl.multiple_of(g * count, count)
        pairs = []
        for dy in range(3):
            for p in range(2):
                at = (dy * 2 + p) * 256
                pairs.append((pooled[p, pl.ds(base + dy * 32, count), :], wc[at : at + 256, :]))
        coarse = jnp.maximum(add_dots(pairs), 0.0).astype(BF16)
        joined = []
        for side in range(2):
            upward = dot(coarse[:, side * 128 : side * 128 + 128], wu[...])
            upward = upward + skip[side, pl.ds(base + 32, count), :].astype(F32)
            joined.append(jnp.maximum(upward, 0.0).astype(BF16))
        for eight in range(LAST_LINES // 8):
            blocks = [
                joined[side][eight * 256 + half * 128 : eight * 256 + half * 128 + 128] for side in range(2) for half in range(2)
            ]
            logits = dot(jnp.concatenate(blocks, axis=1), wh[...]).T
            top = logits.astype(BF16)
            rest = (logits - top.astype(F32)).astype(BF16)
            for half in range(2):
                rows = pl.ds(pl.multiple_of(g * (LAST_LINES * 4), LAST_LINES * 4) + eight * 32 + half * 16, 16)
                for side in range(2):
                    for px in range(2):
                        at = side * 64 + half * 32 + px * 16
                        lanes = slice((side * 2 + px) * 128, (side * 2 + px) * 128 + 128)
                        high[rows, lanes] = top[at : at + 16]
                        low[rows, lanes] = rest[at : at + 16]
        return 0

    lax.fori_loop(0, 64 // LAST_LINES, last_step, 0)

    at, to = iota((128, 512), 0), iota((128, 512), 1)
    same_line = at // 32 == to // 128
    offset = to % 128 - 4 * (at % 32)
    place = jnp.concatenate(
        [jnp.where(same_line & (offset == part), 1.0, 0.0).astype(BF16) for part in range(4)], axis=0
    )
    logits = dot(high[...], place) + dot(low[...], place)
    for line in range(4):
        mixed[line] = logits[:, line * 128 : line * 128 + 128]
    for k in range(3):
        for z in range(2):
            for py in range(2):
                for line in range(4):
                    row = k * 4 + z * 2 + py
                    out[0, k, z, pl.ds(2 * line + py, 16, stride=8), :] = mixed[line, pl.ds(row, 16, stride=16), :]


def on_device(em_volume, neighbours, first_kernel, second_kernel, coarse_kernel, up_kernel, head_kernel):
    own = em_volume[0]
    steps = lax.axis_size("gz")
    prev = lax.ppermute(own, "gz", [(i, i + 1) for i in range(steps - 1)])
    nxt = lax.ppermute(own, "gz", [(i + 1, i) for i in range(steps - 1)])
    limit = pltpu.CompilerParams(vmem_limit_bytes=56 * 2**20)

    shapes = [(256, 2304), (2048, 256), (1536, 256), (128, 256), (1024, 128)]
    weights = pl.pallas_call(
        weights_kernel,
        out_shape=[jax.ShapeDtypeStruct(s, BF16) for s in shapes],
        in_specs=[VMEM] * 5,
        out_specs=[VMEM] * 5,
        scratch_shapes=[
            pltpu.VMEM((896, 128), F32),
            pltpu.VMEM((864, 128), F32),
            pltpu.VMEM((128, 128), F32),
            pltpu.VMEM((28, 8, 128), F32),
        ],
        compiler_params=limit,
        cost_estimate=pl.CostEstimate(flops=10**8, bytes_accessed=4 * 10**6, transcendentals=0),
        name="weights",
    )(
        first_kernel.T,
        jnp.transpose(second_kernel, (2, 0, 1)),
        jnp.transpose(coarse_kernel, (2, 1, 0)),
        jnp.transpose(up_kernel, (0, 2, 1)),
        head_kernel,
    )

    slots = pl.pallas_call(
        pack_kernel,
        out_shape=jax.ShapeDtypeStruct((32, 24, 128), BF16),
        in_specs=[SMEM] + [VMEM] * 3,
        out_specs=VMEM,
        scratch_shapes=[pltpu.VMEM((4, 24, 128), F32)],
        compiler_params=limit,
        name="pack",
    )(neighbours, prev, own, nxt)
    recv = lax.all_to_all(slots, "xy", 0, 0, tiled=True)

    place = jnp.full((1, 1), lax.axis_index("gz"), jnp.int32)
    meta = jnp.concatenate([neighbours, place], axis=1)
    return pl.pallas_call(
        main_kernel,
        out_shape=jax.ShapeDtypeStruct((1, 3, 2, 128, 128), F32),
        in_specs=[SMEM] + [VMEM] * 9,
        out_specs=VMEM,
        scratch_shapes=[
            pltpu.VMEM((8, 144, 128), F32),
            pltpu.VMEM((8, 40, 128), F32),
            pltpu.VMEM((9, 144, 128), F32),
            pltpu.VMEM((68 * 32, 128), BF16),
            pltpu.VMEM((2, 88, 128), F32),
            pltpu.VMEM((67 * 32, 2304), BF16),
            pltpu.VMEM((2, 2, 80, 256), F32),
            pltpu.VMEM((2, LINES * 32, 256), BF16),
            pltpu.VMEM((2, LINES * 32, 256), BF16),
            pltpu.VMEM((256, 512), BF16),
            pltpu.VMEM((256, 512), BF16),
            pltpu.VMEM((4, 256, 128), F32),
        ],
        compiler_params=limit,
        name="layers",
    )(meta, prev, own, nxt, recv, *weights)


def solution(mesh):
    placed = (P("xy", "gz", None, None), P("xy", None), P(), P(), P(), P(), P())
    return jax.shard_map(
        on_device,
        mesh=mesh,
        in_specs=placed,
        out_specs=P("xy", None, "gz", None, None),
        check_vma=False,
    )
```

```python
import jax
import jax.numpy as jnp
from jax import lax
from jax.experimental import pallas as pl
from jax.experimental.pallas import tpu as pltpu
from jax.sharding import PartitionSpec as P

F32 = jnp.float32
BF16 = jnp.bfloat16
LINES = 66
FIRST_LINES, SKIP_LINES, LAST_LINES, LAST_PART = 66, 33, 32, 32
FIRST_OFF = 256.0
SKIP_OFF = 65536.0
VMEM = pl.BlockSpec(memory_space=pltpu.VMEM)
SMEM = pl.BlockSpec(memory_space=pltpu.SMEM)
NT = (((1,), (1,)), ((), ()))


def iota(shape, dim):
    return lax.broadcasted_iota(jnp.int32, shape, dim)


def dot(a, b):
    return jnp.dot(a, b, preferred_element_type=F32)


def dot_nt(a, b):
    return lax.dot_general(a, b, NT, preferred_element_type=F32)


def pack_kernel(nb, place, own, slots, sent, rows):
    sent[...] = own[...]
    lane, line = iota((16, 128), 1), iota((16, 128), 0)
    edge = jnp.where((lane == jnp.where(line < 4, line, 120 + line)) & (line < 8), 1.0, 0.0).astype(BF16)
    planes = jnp.concatenate([own[0], own[1]], axis=0)
    sides = dot_nt(edge, planes)
    for z in range(2):
        at = slice(4 * z, 4 * z + 4)
        rows[0, at, :] = planes[z * 128 : z * 128 + 16].astype(F32)[0:4]
        rows[1, at, :] = planes[z * 128 + 112 : z * 128 + 128].astype(F32)[12:16]
        rows[2, at, :] = sides[0:4, z * 128 : z * 128 + 128]
        rows[3, at, :] = sides[4:8, z * 128 : z * 128 + 128]
    for step in (-1, 0, 1):
        depth = place[0, 0] + step
        for k, strip in enumerate((0, 1, 2, 3, 2, 3, 2, 3)):

            @pl.when((nb[0, k] >= 0) & (depth >= 0) & (depth < 4))
            def _():
                slots[jnp.clip(depth, 0, 3) * 32 + jnp.maximum(nb[0, k], 0)] = rows[strip].astype(BF16)


def weights_kernel(own, first, second, coarse, up, head, wf, ws, wc, wu, wh, taps2, tapsc, part, ups):
    lane = iota((32, 128), 1)
    part[...] = jnp.zeros(part.shape, F32)
    for four in range(7):
        value = jnp.zeros((32, 128), F32)
        for tap in range(4 * four, min(4 * four + 4, 27)):
            part[0:28, 0:28] = second[tap].astype(F32)
            turn = (tap % 4) * 32
            value = value + (pltpu.roll(part[0:32, :], turn, 1) if turn else part[0:32, :])
        turned = jnp.concatenate([value] * 4, axis=0).T
        taps2[four * 128 : four * 128 + 128, :] = turned
    fill = jnp.where(iota((1, 128), 1) % 32 < 28, -SKIP_OFF, 0.0)
    taps2[13 * 32 + 28 : 13 * 32 + 29, :] = fill
    for z in range(4):
        for row in range(4):
            for col in range(4):
                block = (z * 2 + row // 2) * 8 + (col // 2) * 4 + (row % 2) * 2 + col % 2
                for half in range(2):
                    value = jnp.zeros((32, 128), F32)
                    for slot in range(4):
                        dz, dr, dc = z - half, row - slot // 2, col - slot % 2
                        if 0 <= dz < 3 and 0 <= dr < 3 and 0 <= dc < 3:
                            tap = dz * 9 + dr * 3 + dc
                            value = jnp.where(lane // 32 == slot, taps2[tap * 32 : tap * 32 + 32, :], value)
                    ws[block * 32 : block * 32 + 32, half * 128 : half * 128 + 128] = value.astype(BF16)
    part[...] = jnp.zeros(part.shape, F32)
    for tap in range(27):
        part[0:28, 0:56] = coarse[tap].astype(F32)
        tapsc[tap * 32 : tap * 32 + 32, :] = part[0:32, :] + pltpu.roll(part[0:32, :], 64, 1)
    for dy in range(3):
        for z in range(4):
            for col in range(4):
                block = (dy * 4 + z) * 4 + col
                for half in range(2):
                    value = jnp.zeros((32, 128), F32)
                    for slot in range(2):
                        dz, dc = z - slot, col - half
                        if 0 <= dz < 3 and 0 <= dc < 3:
                            tap = dz * 9 + dy * 3 + dc
                            value = jnp.where(lane // 64 == slot, tapsc[tap * 32 : tap * 32 + 32, :], value)
                    wc[block * 32 : block * 32 + 32, half * 128 : half * 128 + 128] = value.astype(BF16)
    part[...] = jnp.zeros(part.shape, F32)
    ups[...] = jnp.zeros(ups.shape, F32)
    ups[:, 0:4, 0:56] = up[...].astype(F32)
    for channel in range(28):
        part[pl.ds(channel, 4, stride=32), :] = ups[channel, 0:4, :]
    mixed = part[...].T[0:64].astype(BF16)
    nothing = jnp.zeros((64, 128), BF16)
    wu[0:64, 0:128] = mixed
    wu[0:64, 128:256] = nothing
    wu[64:128, 0:128] = nothing
    wu[64:128, 128:256] = mixed
    part[...] = jnp.zeros(part.shape, F32)
    part[0:9, 0:28] = first[...].astype(F32)
    by_tap = part[0:16, :]
    by_tap = by_tap + pltpu.roll(by_tap, 32, 1)
    by_tap = by_tap + pltpu.roll(by_tap, 64, 1)
    by_tap = jnp.concatenate([by_tap] * 3, axis=1)
    at, to = iota((256, 384), 0), iota((256, 384), 1)
    row = (at // 128) * 2 + at % 2 - (to // 64) % 2
    col = (at // 2) % 8 - (to // 128) * 2 - (to // 32) % 2
    plane = (at // 16) % 8
    window = jnp.where((row >= 0) & (row < 3) & (col >= 0) & (col < 3), row * 3 + col, -1)
    spread = jnp.zeros((256, 384), F32)
    for tap in range(9):
        spread = jnp.where(window == tap, by_tap[tap : tap + 1, :], spread)
    off = jnp.where(to % 32 < 28, -FIRST_OFF, jnp.where(to % 32 == 28, 1.0, 0.0))
    off = jnp.where((window == 4) & (plane == 6), off, 0.0)
    for z in range(6):
        wf[:, z * 384 : z * 384 + 384] = jnp.where(plane == z, spread, off).astype(BF16)
    part[...] = jnp.zeros(part.shape, F32)
    part[0:3, 0:28] = head[...].astype(F32)
    by_map = part[...].T
    by_map = jnp.concatenate([by_map[0:32]] * 8, axis=0)
    at, to = iota((256, 128), 0), iota((256, 128), 1)
    fits = ((to // 16) % 2 == (at // 32) % 2) & (to % 2 == (at // 64) % 2) & ((to // 2) % 2 == at // 128)
    value = jnp.zeros((256, 128), F32)
    for k in range(3):
        value = jnp.where(fits & ((to % 16) // 4 == k), by_map[:, k : k + 1], value)
    for block in range(4):
        wh[block * 256 : block * 256 + 256, :] = jnp.where(to // 32 == block, value, 0.0).astype(BF16)


def main_kernel(
    nb, depth, prev, own, nxt, recv, wf, ws, wc, wu, wh, out, ext, strips, turned, taps,
    edge_taps, first, edge_mean, pooled, skip, high, low, mixed
):

    strips[...] = jnp.zeros(strips.shape, F32)
    ext[...] = jnp.zeros(ext.shape, F32)
    edge_taps[...] = jnp.zeros(edge_taps.shape, F32)
    for k in range(8):
        have = nb[0, k] >= 0
        for step in range(3):
            near = depth[0, 0] + step - 1
            strip = recv[jnp.clip(near, 0, 3) * 32 + jnp.maximum(nb[0, k], 0)].astype(F32)
            strips[k, 4 + 8 * step : 12 + 8 * step, :] = jnp.where(have & (near >= 0) & (near < 4), strip, 0.0)
        strips[k, 28:32, :] = jnp.full((4, 128), jnp.where(have, 0.0, 1.0), F32)

    for z in range(7):
        if z < 6:
            plane = (prev, own, nxt)[z // 2][z % 2].astype(F32)
            there = (depth[0, 0] > 0, True, depth[0, 0] < 3)[z // 2]
            ext[z, 4:132, :] = jnp.where(there, plane, 0.0)
        ext[z, 0:4, :] = strips[0, 4 * z + 4 : 4 * z + 8, :]
        ext[z, 132:136, :] = strips[1, 4 * z + 4 : 4 * z + 8, :]

    lane = iota((8, 128), 1)
    for b in range(9):
        lines = [ext[z, 16 * b : 16 * b + 16, :] for z in range(8)]
        turned[b, 8:136, :] = jnp.concatenate(lines, axis=0).T
        for start, sides, shift in ((0, (4, 2, 6), 0), (136, (5, 3, 7), 4)):
            value = jnp.zeros((8, 128), F32)
            for z in range(7):
                rows = slice(4 * z + shift, 4 * z + shift + 8)
                line = strips[sides[1], rows, :]
                if b == 0:
                    line = jnp.where(lane >= 124, strips[sides[0], rows, :], line)
                if b == 8:
                    line = jnp.where(lane < 4, strips[sides[2], rows, :], jnp.where(lane >= 124, line, 0.0))
                turn = (16 * z - 16 * b + 4) % 128
                value = jnp.where(lane // 16 == z, pltpu.roll(line, turn, 1) if turn else line, value)
            turned[b, start : start + 8, :] = value
        parts = [
            jnp.concatenate(
                [turned[b, pl.ds(6 + c, 32, stride=4), :], turned[b, pl.ds(2 + c, 2, stride=132), :]], axis=0
            )
            for c in range(8)
        ]
        for bit in (1, 2, 4):
            side = (iota((34, 128), 1) // (2 * bit)) % 2 == 0
            for a in range(8):
                if not a & bit:
                    one, two = parts[a], parts[a + bit]
                    parts[a] = jnp.where(side, one, pltpu.roll(two, 2 * bit, 1))
                    parts[a + bit] = jnp.where(side, pltpu.roll(one, 128 - 2 * bit, 1), two)
        for y in range(8):
            at = 8 * b + y
            if at < 68:
                taps[at * 32 : at * 32 + 32, :] = parts[y][0:32].astype(BF16)
                edge_taps[0, at : at + 1, :] = parts[y][32:33]
                edge_taps[1, at : at + 1, :] = parts[y][33:34]

    at, to = iota((256, 256), 0), iota((256, 256), 1)
    meets = (at // 128 == to // 128) & (at % 32 == to % 32)
    outside = ((depth[0, 0] == 0, False), (False, depth[0, 0] == 3))
    pools, scales = [], []
    for p in range(2):
        low_plane, high_plane = (jnp.where(gone, 0.0, 0.25) for gone in outside[p])
        scales.append(jnp.where(iota((1, 256), 1) < 128, low_plane, high_plane))
        scale = jnp.where(to < 128, jnp.where(outside[p][0], 0.0, 0.25), jnp.where(outside[p][1], 0.0, 0.25))
        pools.append([jnp.where(meets & ((to // 32) % 2 != par), scale, 0.0).astype(BF16) for par in range(2)])

    def add_dots(pairs):
        total = None
        for a, b in pairs:
            term = dot(a, b)
            total = term if total is None else total + term
        return total

    windows = []
    for side in range(2):
        lines = [edge_taps[side, pl.ds(dy, 80), :].astype(BF16) for dy in range(3)]
        windows += [jnp.concatenate(lines[dy : dy + 2], axis=1) for dy in range(2)]
    edges = jnp.maximum(dot(jnp.concatenate(windows, axis=0), wf[...]), 0.0).astype(BF16)
    for p in range(2):
        pairs = []
        for z in range(4):
            for dy in range(2):
                lanes = (2 * p + z) * 384
                west = edges[dy * 80 : dy * 80 + 80, lanes + 128 : lanes + 384]
                east = edges[160 + dy * 80 : 240 + dy * 80, lanes : lanes + 256]
                pairs.append((jnp.concatenate([west, east], axis=0), ws[(z * 2 + dy) * 256 : (z * 2 + dy) * 256 + 256, :]))
        value = jnp.maximum(add_dots(pairs), 0.0).astype(BF16)
        edge_mean[p, 0] = dot(value[0:80], pools[p][1])
        edge_mean[p, 1] = dot(value[80:160], pools[p][0])

    def first_rows(base, count):
        window = jnp.concatenate([taps[pl.ds(base, count), :], taps[pl.ds(base + 32, count), :]], axis=1)
        for n in range(0, 2304, 256):
            first[pl.ds(base, count), n : n + 256] = jnp.maximum(dot(window, wf[:, n : n + 256]), 0.0).astype(BF16)

    def first_step(g, _):
        first_rows(pl.multiple_of(g * (FIRST_LINES * 32), FIRST_LINES * 32), FIRST_LINES * 32)
        return 0

    lax.fori_loop(0, 66 // FIRST_LINES, first_step, 0)
    first_rows(2112, 32)

    def skip_step(g, _):
        count = SKIP_LINES * 32
        base = pl.multiple_of(g * count, count)
        group = (iota((count, 256), 1) // 32) % 4
        line_row, line_group = iota((32, 256), 0), (iota((32, 256), 1) // 32) % 4
        for p in range(2):
            values = []
            for par in range(2):
                pairs = []
                for z in range(4):
                    for dy in range(2):
                        lanes = (2 * p + z) * 384 + par * 128
                        at = (z * 2 + dy) * 256
                        pairs.append((first[pl.ds(base + dy * 32, count), lanes : lanes + 256], ws[at : at + 256, :]))
                value = jnp.maximum(add_dots(pairs), 0.0).astype(BF16)
                skip[par, pl.ds(base, count), p * 128 : p * 128 + 128] = value[:, 128 - p * 128 : 256 - p * 128]
                values.append(value)
            sums = []
            for value in values:
                value = value.astype(F32)
                halves = []
                for half in (value[:, 0:128], value[:, 128:256]):
                    half = half + pltpu.roll(half, 32, 1)
                    halves.append(half + pltpu.roll(half, 64, 1))
                sums.append(jnp.concatenate(halves, axis=1))
            mean = jnp.where(group % 2 == 1, sums[0], sums[1]) * scales[p]
            before, after = pltpu.roll(mean, 1, 0), pltpu.roll(mean, count - 1, 0)
            mean = jnp.where(group == 0, before, jnp.where(group == 3, after, mean))
            for y in range(SKIP_LINES):
                line = mean[y * 32 : y * 32 + 32]
                west = edge_mean[p, 0, pl.ds(g * SKIP_LINES + y, 1), :]
                east = edge_mean[p, 1, pl.ds(g * SKIP_LINES + y, 1), :]
                line = jnp.where((line_row == 0) & (line_group == 0), west, line)
                line = jnp.where((line_row == 31) & (line_group == 3), east, line)
                pooled[p, pl.ds(base + y * 32, 32), :] = line.astype(BF16)
        return 0

    lax.fori_loop(0, 66 // SKIP_LINES, skip_step, 0)


    def last_rows(base, top_row):
        count = LAST_PART * 32
        pairs = []
        for dy in range(3):
            for p in range(2):
                at = (dy * 2 + p) * 256
                pairs.append((pooled[p, pl.ds(base + dy * 32, count), :], wc[at : at + 256, :]))
        coarse = jnp.maximum(add_dots(pairs), 0.0).astype(BF16)
        joined = []
        for side in range(2):
            upward = dot(coarse[:, side * 128 : side * 128 + 128], wu[...])
            upward = upward + skip[side, pl.ds(base + 32, count), :].astype(F32)
            joined.append(jnp.maximum(upward, 0.0).astype(BF16))
        eights = range(0, count, 256)
        blocks = [
            jnp.concatenate([joined[side][at + half * 128 : at + half * 128 + 128] for at in eights], axis=0)
            for side in range(2)
            for half in range(2)
        ]
        mapped = dot(jnp.concatenate(blocks, axis=1), wh[...])
        for eight in range(LAST_PART // 8):
            logits = mapped[eight * 128 : eight * 128 + 128].T
            top = logits.astype(BF16)
            rest = (logits - top.astype(F32)).astype(BF16)
            for half in range(2):
                rows = pl.ds(top_row + eight * 32 + half * 16, 16)
                for side in range(2):
                    for px in range(2):
                        at = side * 64 + half * 32 + px * 16
                        lanes = slice((side * 2 + px) * 128, (side * 2 + px) * 128 + 128)
                        high[rows, lanes] = top[at : at + 16]
                        low[rows, lanes] = rest[at : at + 16]

    def last_step(g, _):
        base = pl.multiple_of(g * (LAST_LINES * 32), LAST_LINES * 32)
        top_row = pl.multiple_of(g * (LAST_LINES * 4), LAST_LINES * 4)
        for part in range(LAST_LINES // LAST_PART):
            last_rows(base + part * LAST_PART * 32, top_row + part * LAST_PART * 4)
        return 0

    lax.fori_loop(0, 64 // LAST_LINES, last_step, 0)

    at, to = iota((128, 512), 0), iota((128, 512), 1)
    same_line = at // 32 == to // 128
    offset = to % 128 - 4 * (at % 32)
    place = jnp.concatenate(
        [jnp.where(same_line & (offset == part), 1.0, 0.0).astype(BF16) for part in range(4)], axis=0
    )
    logits = dot(high[...], place) + dot(low[...], place)
    for line in range(4):
        mixed[line] = logits[:, line * 128 : line * 128 + 128]
    for k in range(3):
        for z in range(2):
            for py in range(2):
                for line in range(4):
                    row = k * 4 + z * 2 + py
                    out[0, k, z, pl.ds(2 * line + py, 16, stride=8), :] = mixed[line, pl.ds(row, 16, stride=16), :]


def on_device(em_volume, neighbours, first_kernel, second_kernel, coarse_kernel, up_kernel, head_kernel):
    own = em_volume[0]
    steps = lax.axis_size("gz")
    place = jnp.full((1, 1), lax.axis_index("gz"), jnp.int32)
    limit = pltpu.CompilerParams(vmem_limit_bytes=56 * 2**20)
    image = jax.ShapeDtypeStruct(own.shape, BF16)

    slots, sent = pl.pallas_call(
        pack_kernel,
        out_shape=[jax.ShapeDtypeStruct((128, 8, 128), BF16), image],
        in_specs=[SMEM, SMEM, VMEM],
        out_specs=[VMEM, VMEM],
        scratch_shapes=[pltpu.VMEM((4, 8, 128), F32)],
        compiler_params=limit,
        name="pack",
    )(neighbours, place, own)
    recv = lax.all_to_all(slots, ("gz", "xy"), 0, 0, tiled=True)
    prev = lax.ppermute(sent, "gz", [(i, (i + 1) % steps) for i in range(steps)])
    nxt = lax.ppermute(sent, "gz", [((i + 1) % steps, i) for i in range(steps)])

    shapes = [(256, 2304), (2048, 256), (1536, 256), (128, 256), (1024, 128)]
    weights = pl.pallas_call(
        weights_kernel,
        out_shape=[jax.ShapeDtypeStruct(s, BF16) for s in shapes],
        in_specs=[VMEM] * 6,
        out_specs=[VMEM] * 5,
        scratch_shapes=[
            pltpu.VMEM((896, 128), F32),
            pltpu.VMEM((864, 128), F32),
            pltpu.VMEM((128, 128), F32),
            pltpu.VMEM((28, 8, 128), F32),
        ],
        compiler_params=limit,
        cost_estimate=pl.CostEstimate(flops=10**8, bytes_accessed=4 * 10**6, transcendentals=0),
        name="weights",
    )(
        sent,
        first_kernel.T,
        jnp.transpose(second_kernel, (2, 0, 1)),
        jnp.transpose(coarse_kernel, (2, 1, 0)),
        jnp.transpose(up_kernel, (0, 2, 1)),
        head_kernel,
    )

    return pl.pallas_call(
        main_kernel,
        out_shape=jax.ShapeDtypeStruct((1, 3, 2, 128, 128), F32),
        in_specs=[SMEM] * 2 + [VMEM] * 9,
        out_specs=VMEM,
        scratch_shapes=[
            pltpu.VMEM((8, 144, 128), F32),
            pltpu.VMEM((8, 40, 128), F32),
            pltpu.VMEM((9, 144, 128), F32),
            pltpu.VMEM((68 * 32, 128), BF16),
            pltpu.VMEM((2, 88, 128), F32),
            pltpu.VMEM((67 * 32, 2304), BF16),
            pltpu.VMEM((2, 2, 80, 256), F32),
            pltpu.VMEM((2, LINES * 32, 256), BF16),
            pltpu.VMEM((2, LINES * 32, 256), BF16),
            pltpu.VMEM((256, 512), BF16),
            pltpu.VMEM((256, 512), BF16),
            pltpu.VMEM((4, 256, 128), F32),
        ],
        compiler_params=limit,
        name="layers",
    )(neighbours, place, prev, own, nxt, recv, *weights)


def solution(mesh):
    placed = (P("xy", "gz", None, None), P("xy", None), P(), P(), P(), P(), P())
    return jax.shard_map(
        on_device,
        mesh=mesh,
        in_specs=placed,
        out_specs=P("xy", None, "gz", None, None),
        check_vma=False,
    )
```

```python
import jax
import jax.numpy as jnp
from jax import lax
from jax.experimental import pallas as pl
from jax.experimental.pallas import tpu as pltpu
from jax.sharding import PartitionSpec as P

F32 = jnp.float32
BF16 = jnp.bfloat16
LINES = 66
FIRST_AFTER = (1, 3, 5, 8)
SKIP_STEPS = (22, 22, 22)
LAST_STEPS = (32, 32)
FIRST_OFF = 256.0
SKIP_OFF = 65536.0
VMEM = pl.BlockSpec(memory_space=pltpu.VMEM)
SMEM = pl.BlockSpec(memory_space=pltpu.SMEM)
NT = (((1,), (1,)), ((), ()))


def iota(shape, dim):
    return lax.broadcasted_iota(jnp.int32, shape, dim)


def dot(a, b):
    return jnp.dot(a, b, preferred_element_type=F32)


def dot_nt(a, b):
    return lax.dot_general(a, b, NT, preferred_element_type=F32)


def pack_kernel(nb, place, own, slots, sent, rows):
    sent[...] = own[...]
    lane, line = iota((16, 128), 1), iota((16, 128), 0)
    edge = jnp.where((lane == jnp.where(line < 4, line, 120 + line)) & (line < 8), 1.0, 0.0).astype(BF16)
    planes = jnp.concatenate([own[0], own[1]], axis=0)
    sides = dot_nt(edge, planes)
    for z in range(2):
        at = slice(4 * z, 4 * z + 4)
        rows[0, at, :] = planes[z * 128 : z * 128 + 16].astype(F32)[0:4]
        rows[1, at, :] = planes[z * 128 + 112 : z * 128 + 128].astype(F32)[12:16]
        rows[2, at, :] = sides[0:4, z * 128 : z * 128 + 128]
        rows[3, at, :] = sides[4:8, z * 128 : z * 128 + 128]
    for step in (-1, 0, 1):
        depth = place[0, 0] + step
        for k, strip in enumerate((0, 1, 2, 3, 2, 3, 2, 3)):

            @pl.when((nb[0, k] >= 0) & (depth >= 0) & (depth < 4))
            def _():
                slots[jnp.clip(depth, 0, 3) * 32 + jnp.maximum(nb[0, k], 0)] = rows[strip].astype(BF16)


def weights_kernel(own, first, second, coarse, up, head, wf, ws, wc, wu, wh, taps2, tapsc, part, ups):
    lane = iota((32, 128), 1)
    part[...] = jnp.zeros(part.shape, F32)
    for four in range(7):
        value = jnp.zeros((32, 128), F32)
        for tap in range(4 * four, min(4 * four + 4, 27)):
            part[0:28, 0:28] = second[tap].astype(F32)
            turn = (tap % 4) * 32
            value = value + (pltpu.roll(part[0:32, :], turn, 1) if turn else part[0:32, :])
        turned = jnp.concatenate([value] * 4, axis=0).T
        taps2[four * 128 : four * 128 + 128, :] = turned
    fill = jnp.where(iota((1, 128), 1) % 32 < 28, -SKIP_OFF, 0.0)
    taps2[13 * 32 + 28 : 13 * 32 + 29, :] = fill
    for z in range(4):
        for row in range(4):
            for col in range(4):
                block = (z * 2 + row // 2) * 8 + (col // 2) * 4 + (row % 2) * 2 + col % 2
                for half in range(2):
                    value = jnp.zeros((32, 128), F32)
                    for slot in range(4):
                        dz, dr, dc = z - half, row - slot // 2, col - slot % 2
                        if 0 <= dz < 3 and 0 <= dr < 3 and 0 <= dc < 3:
                            tap = dz * 9 + dr * 3 + dc
                            value = jnp.where(lane // 32 == slot, taps2[tap * 32 : tap * 32 + 32, :], value)
                    ws[block * 32 : block * 32 + 32, half * 128 : half * 128 + 128] = value.astype(BF16)
    part[...] = jnp.zeros(part.shape, F32)
    for tap in range(27):
        part[0:28, 0:56] = coarse[tap].astype(F32)
        tapsc[tap * 32 : tap * 32 + 32, :] = part[0:32, :] + pltpu.roll(part[0:32, :], 64, 1)
    for dy in range(3):
        for z in range(4):
            for col in range(4):
                block = (dy * 4 + z) * 4 + col
                for half in range(2):
                    value = jnp.zeros((32, 128), F32)
                    for slot in range(2):
                        dz, dc = z - slot, col - half
                        if 0 <= dz < 3 and 0 <= dc < 3:
                            tap = dz * 9 + dy * 3 + dc
                            value = jnp.where(lane // 64 == slot, tapsc[tap * 32 : tap * 32 + 32, :], value)
                    wc[block * 32 : block * 32 + 32, half * 128 : half * 128 + 128] = value.astype(BF16)
    part[...] = jnp.zeros(part.shape, F32)
    ups[...] = jnp.zeros(ups.shape, F32)
    ups[:, 0:4, 0:56] = up[...].astype(F32)
    for channel in range(28):
        part[pl.ds(channel, 4, stride=32), :] = ups[channel, 0:4, :]
    mixed = part[...].T[0:64].astype(BF16)
    nothing = jnp.zeros((64, 128), BF16)
    wu[0:64, 0:128] = mixed
    wu[0:64, 128:256] = nothing
    wu[64:128, 0:128] = nothing
    wu[64:128, 128:256] = mixed
    part[...] = jnp.zeros(part.shape, F32)
    part[0:9, 0:28] = first[...].astype(F32)
    by_tap = part[0:16, :]
    by_tap = by_tap + pltpu.roll(by_tap, 32, 1)
    by_tap = by_tap + pltpu.roll(by_tap, 64, 1)
    by_tap = jnp.concatenate([by_tap] * 3, axis=1)
    at, to = iota((256, 384), 0), iota((256, 384), 1)
    row = (at // 128) * 2 + at % 2 - (to // 64) % 2
    col = (at // 2) % 8 - (to // 128) * 2 - (to // 32) % 2
    plane = (at // 16) % 8
    window = jnp.where((row >= 0) & (row < 3) & (col >= 0) & (col < 3), row * 3 + col, -1)
    spread = jnp.zeros((256, 384), F32)
    for tap in range(9):
        spread = jnp.where(window == tap, by_tap[tap : tap + 1, :], spread)
    off = jnp.where(to % 32 < 28, -FIRST_OFF, jnp.where(to % 32 == 28, 1.0, 0.0))
    off = jnp.where((window == 4) & (plane == 6), off, 0.0)
    for z in range(6):
        wf[:, z * 384 : z * 384 + 384] = jnp.where(plane == z, spread, off).astype(BF16)
    part[...] = jnp.zeros(part.shape, F32)
    part[0:3, 0:28] = head[...].astype(F32)
    by_map = part[...].T
    by_map = jnp.concatenate([by_map[0:32]] * 8, axis=0)
    at, to = iota((256, 128), 0), iota((256, 128), 1)
    fits = ((to // 16) % 2 == (at // 32) % 2) & (to % 2 == (at // 64) % 2) & ((to // 2) % 2 == at // 128)
    value = jnp.zeros((256, 128), F32)
    for k in range(3):
        value = jnp.where(fits & ((to % 16) // 4 == k), by_map[:, k : k + 1], value)
    for block in range(4):
        wh[block * 256 : block * 256 + 256, :] = jnp.where(to // 32 == block, value, 0.0).astype(BF16)


def main_kernel(
    nb, depth, prev, own, nxt, recv, wf, ws, wc, wu, wh, out, ext, strips, turned, taps,
    edge_taps, first, edge_mean, pooled, skip, high, low, mixed
):

    strips[...] = jnp.zeros(strips.shape, F32)
    ext[...] = jnp.zeros(ext.shape, F32)
    edge_taps[...] = jnp.zeros(edge_taps.shape, F32)
    for k in range(8):
        have = nb[0, k] >= 0
        for step in range(3):
            near = depth[0, 0] + step - 1
            strip = recv[jnp.clip(near, 0, 3) * 32 + jnp.maximum(nb[0, k], 0)].astype(F32)
            strips[k, 4 + 8 * step : 12 + 8 * step, :] = jnp.where(have & (near >= 0) & (near < 4), strip, 0.0)
        strips[k, 28:32, :] = jnp.full((4, 128), jnp.where(have, 0.0, 1.0), F32)

    for z in range(7):
        if z < 6:
            plane = (prev, own, nxt)[z // 2][z % 2].astype(F32)
            there = (depth[0, 0] > 0, True, depth[0, 0] < 3)[z // 2]
            ext[z, 4:132, :] = jnp.where(there, plane, 0.0)
        ext[z, 0:4, :] = strips[0, 4 * z + 4 : 4 * z + 8, :]
        ext[z, 132:136, :] = strips[1, 4 * z + 4 : 4 * z + 8, :]

    lane = iota((8, 128), 1)
    def first_rows(base, count):
        window = jnp.concatenate([taps[pl.ds(base, count), :], taps[pl.ds(base + 32, count), :]], axis=1)
        for n in range(0, 2304, 256):
            first[pl.ds(base, count), n : n + 256] = jnp.maximum(dot(window, wf[:, n : n + 256]), 0.0).astype(BF16)

    done = 0
    for b in range(9):
        lines = [ext[z, 16 * b : 16 * b + 16, :] for z in range(8)]
        turned[b, 8:136, :] = jnp.concatenate(lines, axis=0).T
        for start, sides, shift in ((0, (4, 2, 6), 0), (136, (5, 3, 7), 4)):
            value = jnp.zeros((8, 128), F32)
            for z in range(7):
                rows = slice(4 * z + shift, 4 * z + shift + 8)
                line = strips[sides[1], rows, :]
                if b == 0:
                    line = jnp.where(lane >= 124, strips[sides[0], rows, :], line)
                if b == 8:
                    line = jnp.where(lane < 4, strips[sides[2], rows, :], jnp.where(lane >= 124, line, 0.0))
                turn = (16 * z - 16 * b + 4) % 128
                value = jnp.where(lane // 16 == z, pltpu.roll(line, turn, 1) if turn else line, value)
            turned[b, start : start + 8, :] = value
        parts = [
            jnp.concatenate(
                [turned[b, pl.ds(6 + c, 32, stride=4), :], turned[b, pl.ds(2 + c, 2, stride=132), :]], axis=0
            )
            for c in range(8)
        ]
        for bit in (1, 2, 4):
            side = (iota((34, 128), 1) // (2 * bit)) % 2 == 0
            for a in range(8):
                if not a & bit:
                    one, two = parts[a], parts[a + bit]
                    parts[a] = jnp.where(side, one, pltpu.roll(two, 2 * bit, 1))
                    parts[a + bit] = jnp.where(side, pltpu.roll(one, 128 - 2 * bit, 1), two)
        for y in range(8):
            at = 8 * b + y
            if at < 68:
                taps[at * 32 : at * 32 + 32, :] = parts[y][0:32].astype(BF16)
                edge_taps[0, at : at + 1, :] = parts[y][32:33]
                edge_taps[1, at : at + 1, :] = parts[y][33:34]
        if b in FIRST_AFTER:
            ready = min(8 * b + 7, 67)
            first_rows(done * 32, (ready - done) * 32)
            done = ready

    at, to = iota((256, 256), 0), iota((256, 256), 1)
    meets = (at // 128 == to // 128) & (at % 32 == to % 32)
    outside = ((depth[0, 0] == 0, False), (False, depth[0, 0] == 3))
    pools, scales = [], []
    for p in range(2):
        low_plane, high_plane = (jnp.where(gone, 0.0, 0.25) for gone in outside[p])
        scales.append((low_plane, high_plane))
        scale = jnp.where(to < 128, jnp.where(outside[p][0], 0.0, 0.25), jnp.where(outside[p][1], 0.0, 0.25))
        pools.append([jnp.where(meets & ((to // 32) % 2 != par), scale, 0.0).astype(BF16) for par in range(2)])

    def add_dots(pairs):
        total = None
        for a, b in pairs:
            term = dot(a, b)
            total = term if total is None else total + term
        return total

    windows = []
    for side in range(2):
        lines = [edge_taps[side, pl.ds(dy, 80), :].astype(BF16) for dy in range(3)]
        windows += [jnp.concatenate(lines[dy : dy + 2], axis=1) for dy in range(2)]
    edges = jnp.maximum(dot(jnp.concatenate(windows, axis=0), wf[...]), 0.0).astype(BF16)
    for p in range(2):
        pairs = []
        for z in range(4):
            for dy in range(2):
                lanes = (2 * p + z) * 384
                west = edges[dy * 80 : dy * 80 + 80, lanes + 128 : lanes + 384]
                east = edges[160 + dy * 80 : 240 + dy * 80, lanes : lanes + 256]
                pairs.append((jnp.concatenate([west, east], axis=0), ws[(z * 2 + dy) * 256 : (z * 2 + dy) * 256 + 256, :]))
        value = jnp.maximum(add_dots(pairs), 0.0).astype(BF16)
        edge_mean[p, 0] = dot(value[0:80], pools[p][1])
        edge_mean[p, 1] = dot(value[80:160], pools[p][0])

    group = iota((1, 128), 1) // 32
    tile_row, tile_group = iota((8, 256), 0), (iota((8, 256), 1) // 32) % 4
    at_west, at_east = (tile_row == 0) & (tile_group == 0), (tile_row == 7) & (tile_group == 3)

    def skip_rows(top, lines):
        base, count = top * 32, lines * 32
        for p in range(2):
            values = []
            for par in range(2):
                pairs = []
                for z in range(4):
                    for dy in range(2):
                        lanes = (2 * p + z) * 384 + par * 128
                        at = (z * 2 + dy) * 256
                        pairs.append((first[pl.ds(base + dy * 32, count), lanes : lanes + 256], ws[at : at + 256, :]))
                value = jnp.maximum(add_dots(pairs), 0.0).astype(BF16)
                skip[par, pl.ds(base, count), p * 128 : p * 128 + 128] = value[:, 128 - p * 128 : 256 - p * 128]
                values.append(value)
            halves = []
            for half in range(2):
                sums = []
                for value in values:
                    part = value[:, half * 128 : half * 128 + 128].astype(F32)
                    part = part + pltpu.roll(part, 32, 1)
                    sums.append(part + pltpu.roll(part, 64, 1))
                mean = jnp.where(group % 2 == 1, sums[0], sums[1]) * scales[p][half]
                before, after = pltpu.roll(mean, 1, 0), pltpu.roll(mean, count - 1, 0)
                halves.append(jnp.where(group == 0, before, jnp.where(group == 3, after, mean)))
            mean = jnp.concatenate(halves, axis=1)
            for y in range(lines):
                west = edge_mean[p, 0, top + y : top + y + 1, :]
                east = edge_mean[p, 1, top + y : top + y + 1, :]
                line = [mean[y * 32 + at : y * 32 + at + 8] for at in range(0, 32, 8)]
                line[0] = jnp.where(at_west, west, line[0])
                line[3] = jnp.where(at_east, east, line[3])
                pooled[p, pl.ds(base + y * 32, 32), :] = jnp.concatenate(line, axis=0).astype(BF16)

    top = 0
    for lines in SKIP_STEPS:
        skip_rows(top, lines)
        top += lines


    def last_rows(top, lines):
        base, count = top * 32, lines * 32
        pairs = []
        for dy in range(3):
            for p in range(2):
                at = (dy * 2 + p) * 256
                pairs.append((pooled[p, pl.ds(base + dy * 32, count), :], wc[at : at + 256, :]))
        coarse = jnp.maximum(add_dots(pairs), 0.0).astype(BF16)
        joined = []
        for side in range(2):
            upward = dot(coarse[:, side * 128 : side * 128 + 128], wu[...])
            upward = upward + skip[side, pl.ds(base + 32, count), :].astype(F32)
            joined.append(jnp.maximum(upward, 0.0).astype(BF16))
        eights = range(0, count, 256)
        blocks = [
            jnp.concatenate([joined[side][at + half * 128 : at + half * 128 + 128] for at in eights], axis=0)
            for side in range(2)
            for half in range(2)
        ]
        mapped = dot(jnp.concatenate(blocks, axis=1), wh[...])
        for eight in range(lines // 8):
            logits = mapped[eight * 128 : eight * 128 + 128].T
            rounded = logits.astype(BF16)
            rest = (logits - rounded.astype(F32)).astype(BF16)
            for half in range(2):
                rows = pl.ds(top * 4 + eight * 32 + half * 16, 16)
                for side in range(2):
                    for px in range(2):
                        at = side * 64 + half * 32 + px * 16
                        lanes = slice((side * 2 + px) * 128, (side * 2 + px) * 128 + 128)
                        high[rows, lanes] = rounded[at : at + 16]
                        low[rows, lanes] = rest[at : at + 16]

    top = 0
    for lines in LAST_STEPS:
        last_rows(top, lines)
        top += lines

    at, to = iota((128, 512), 0), iota((128, 512), 1)
    same_line = at // 32 == to // 128
    offset = to % 128 - 4 * (at % 32)
    place = jnp.concatenate(
        [jnp.where(same_line & (offset == part), 1.0, 0.0).astype(BF16) for part in range(4)], axis=0
    )
    logits = dot(high[...], place) + dot(low[...], place)
    for line in range(4):
        mixed[line] = logits[:, line * 128 : line * 128 + 128]
    for k in range(3):
        for z in range(2):
            for py in range(2):
                for line in range(4):
                    row = k * 4 + z * 2 + py
                    out[0, k, z, pl.ds(2 * line + py, 16, stride=8), :] = mixed[line, pl.ds(row, 16, stride=16), :]


def on_device(em_volume, neighbours, first_kernel, second_kernel, coarse_kernel, up_kernel, head_kernel):
    own = em_volume[0]
    steps = lax.axis_size("gz")
    place = jnp.full((1, 1), lax.axis_index("gz"), jnp.int32)
    limit = pltpu.CompilerParams(vmem_limit_bytes=56 * 2**20)
    image = jax.ShapeDtypeStruct(own.shape, BF16)

    slots, sent = pl.pallas_call(
        pack_kernel,
        out_shape=[jax.ShapeDtypeStruct((128, 8, 128), BF16), image],
        in_specs=[SMEM, SMEM, VMEM],
        out_specs=[VMEM, VMEM],
        scratch_shapes=[pltpu.VMEM((4, 8, 128), F32)],
        compiler_params=limit,
        name="pack",
    )(neighbours, place, own)
    recv = lax.all_to_all(slots, ("gz", "xy"), 0, 0, tiled=True)
    prev = lax.ppermute(sent, "gz", [(i, (i + 1) % steps) for i in range(steps)])
    nxt = lax.ppermute(sent, "gz", [((i + 1) % steps, i) for i in range(steps)])

    shapes = [(256, 2304), (2048, 256), (1536, 256), (128, 256), (1024, 128)]
    weights = pl.pallas_call(
        weights_kernel,
        out_shape=[jax.ShapeDtypeStruct(s, BF16) for s in shapes],
        in_specs=[VMEM] * 6,
        out_specs=[VMEM] * 5,
        scratch_shapes=[
            pltpu.VMEM((896, 128), F32),
            pltpu.VMEM((864, 128), F32),
            pltpu.VMEM((128, 128), F32),
            pltpu.VMEM((28, 8, 128), F32),
        ],
        compiler_params=limit,
        cost_estimate=pl.CostEstimate(flops=10**8, bytes_accessed=4 * 10**6, transcendentals=0),
        name="weights",
    )(
        sent,
        first_kernel.T,
        jnp.transpose(second_kernel, (2, 0, 1)),
        jnp.transpose(coarse_kernel, (2, 1, 0)),
        jnp.transpose(up_kernel, (0, 2, 1)),
        head_kernel,
    )

    return pl.pallas_call(
        main_kernel,
        out_shape=jax.ShapeDtypeStruct((1, 3, 2, 128, 128), F32),
        in_specs=[SMEM] * 2 + [VMEM] * 9,
        out_specs=VMEM,
        scratch_shapes=[
            pltpu.VMEM((8, 144, 128), F32),
            pltpu.VMEM((8, 40, 128), F32),
            pltpu.VMEM((9, 144, 128), F32),
            pltpu.VMEM((68 * 32, 128), BF16),
            pltpu.VMEM((2, 88, 128), F32),
            pltpu.VMEM((67 * 32, 2304), BF16),
            pltpu.VMEM((2, 2, 80, 256), F32),
            pltpu.VMEM((2, LINES * 32, 256), BF16),
            pltpu.VMEM((2, LINES * 32, 256), BF16),
            pltpu.VMEM((256, 512), BF16),
            pltpu.VMEM((256, 512), BF16),
            pltpu.VMEM((4, 256, 128), F32),
        ],
        compiler_params=limit,
        name="layers",
    )(neighbours, place, prev, own, nxt, recv, *weights)


def solution(mesh):
    placed = (P("xy", "gz", None, None), P("xy", None), P(), P(), P(), P(), P())
    return jax.shard_map(
        on_device,
        mesh=mesh,
        in_specs=placed,
        out_specs=P("xy", None, "gz", None, None),
        check_vma=False,
    )
```

```python
import jax
import jax.numpy as jnp
from jax import lax
from jax.experimental import pallas as pl
from jax.experimental.pallas import tpu as pltpu
from jax.sharding import PartitionSpec as P

F32 = jnp.float32
BF16 = jnp.bfloat16
LINES = 66
FIRST_AFTER = (1, 3, 5, 8)
SKIP_STEPS = (11,) * 6
LAST_STEPS = (((0, 16), 16), ((32, 48), 16))
FIRST_OFF = 256.0
SKIP_OFF = 65536.0
VMEM = pl.BlockSpec(memory_space=pltpu.VMEM)
SMEM = pl.BlockSpec(memory_space=pltpu.SMEM)
NT = (((1,), (1,)), ((), ()))


def iota(shape, dim):
    return lax.broadcasted_iota(jnp.int32, shape, dim)


def dot(a, b):
    return jnp.dot(a, b, preferred_element_type=F32)


def dot_nt(a, b):
    return lax.dot_general(a, b, NT, preferred_element_type=F32)


def pack_kernel(nb, place, own, slots, sent, rows):
    sent[...] = own[...]
    lane, line = iota((16, 128), 1), iota((16, 128), 0)
    edge = jnp.where((lane == jnp.where(line < 4, line, 120 + line)) & (line < 8), 1.0, 0.0).astype(BF16)
    planes = jnp.concatenate([own[0], own[1]], axis=0)
    sides = dot_nt(edge, planes)
    for z in range(2):
        at = slice(4 * z, 4 * z + 4)
        rows[0, at, :] = planes[z * 128 : z * 128 + 16].astype(F32)[0:4]
        rows[1, at, :] = planes[z * 128 + 112 : z * 128 + 128].astype(F32)[12:16]
        rows[2, at, :] = sides[0:4, z * 128 : z * 128 + 128]
        rows[3, at, :] = sides[4:8, z * 128 : z * 128 + 128]
    for step in (-1, 0, 1):
        depth = place[0, 0] + step
        for k, strip in enumerate((0, 1, 2, 3, 2, 3, 2, 3)):

            @pl.when((nb[0, k] >= 0) & (depth >= 0) & (depth < 4))
            def _():
                slots[jnp.clip(depth, 0, 3) * 32 + jnp.maximum(nb[0, k], 0)] = rows[strip].astype(BF16)


def weights_kernel(own, first, second, coarse, up, head, wf, ws, wc, wu, wh, taps2, tapsc, part, ups):
    lane = iota((32, 128), 1)
    part[...] = jnp.zeros(part.shape, F32)
    for four in range(7):
        value = jnp.zeros((32, 128), F32)
        for tap in range(4 * four, min(4 * four + 4, 27)):
            part[0:28, 0:28] = second[tap].astype(F32)
            turn = (tap % 4) * 32
            value = value + (pltpu.roll(part[0:32, :], turn, 1) if turn else part[0:32, :])
        turned = jnp.concatenate([value] * 4, axis=0).T
        taps2[four * 128 : four * 128 + 128, :] = turned
    fill = jnp.where(iota((1, 128), 1) % 32 < 28, -SKIP_OFF, 0.0)
    taps2[13 * 32 + 28 : 13 * 32 + 29, :] = fill
    for z in range(4):
        for row in range(4):
            for col in range(4):
                block = (z * 2 + row // 2) * 8 + (col // 2) * 4 + (row % 2) * 2 + col % 2
                for half in range(2):
                    value = jnp.zeros((32, 128), F32)
                    for slot in range(4):
                        dz, dr, dc = z - half, row - slot // 2, col - slot % 2
                        if 0 <= dz < 3 and 0 <= dr < 3 and 0 <= dc < 3:
                            tap = dz * 9 + dr * 3 + dc
                            value = jnp.where(lane // 32 == slot, taps2[tap * 32 : tap * 32 + 32, :], value)
                    ws[block * 32 : block * 32 + 32, half * 128 : half * 128 + 128] = value.astype(BF16)
    part[...] = jnp.zeros(part.shape, F32)
    for tap in range(27):
        part[0:28, 0:56] = coarse[tap].astype(F32)
        tapsc[tap * 32 : tap * 32 + 32, :] = part[0:32, :] + pltpu.roll(part[0:32, :], 64, 1)
    for dy in range(3):
        for z in range(4):
            for col in range(4):
                block = (dy * 4 + z) * 4 + col
                for half in range(2):
                    value = jnp.zeros((32, 128), F32)
                    for slot in range(2):
                        dz, dc = z - slot, col - half
                        if 0 <= dz < 3 and 0 <= dc < 3:
                            tap = dz * 9 + dy * 3 + dc
                            value = jnp.where(lane // 64 == slot, tapsc[tap * 32 : tap * 32 + 32, :], value)
                    wc[block * 32 : block * 32 + 32, half * 128 : half * 128 + 128] = value.astype(BF16)
    part[...] = jnp.zeros(part.shape, F32)
    ups[...] = jnp.zeros(ups.shape, F32)
    ups[:, 0:4, 0:56] = up[...].astype(F32)
    for channel in range(28):
        part[pl.ds(channel, 4, stride=32), :] = ups[channel, 0:4, :]
    mixed = part[...].T[0:64].astype(BF16)
    nothing = jnp.zeros((64, 128), BF16)
    wu[0:64, 0:128] = mixed
    wu[0:64, 128:256] = nothing
    wu[64:128, 0:128] = nothing
    wu[64:128, 128:256] = mixed
    part[...] = jnp.zeros(part.shape, F32)
    part[0:9, 0:28] = first[...].astype(F32)
    by_tap = part[0:16, :]
    by_tap = by_tap + pltpu.roll(by_tap, 32, 1)
    by_tap = by_tap + pltpu.roll(by_tap, 64, 1)
    by_tap = jnp.concatenate([by_tap] * 3, axis=1)
    at, to = iota((256, 384), 0), iota((256, 384), 1)
    row = (at // 128) * 2 + at % 2 - (to // 64) % 2
    col = (at // 2) % 8 - (to // 128) * 2 - (to // 32) % 2
    plane = (at // 16) % 8
    window = jnp.where((row >= 0) & (row < 3) & (col >= 0) & (col < 3), row * 3 + col, -1)
    spread = jnp.zeros((256, 384), F32)
    for tap in range(9):
        spread = jnp.where(window == tap, by_tap[tap : tap + 1, :], spread)
    off = jnp.where(to % 32 < 28, -FIRST_OFF, jnp.where(to % 32 == 28, 1.0, 0.0))
    off = jnp.where((window == 4) & (plane == 6), off, 0.0)
    for z in range(6):
        wf[:, z * 384 : z * 384 + 384] = jnp.where(plane == z, spread, off).astype(BF16)
    part[...] = jnp.zeros(part.shape, F32)
    part[0:3, 0:28] = head[...].astype(F32)
    by_map = part[...].T
    by_map = jnp.concatenate([by_map[0:32]] * 8, axis=0)
    at, to = iota((256, 128), 0), iota((256, 128), 1)
    fits = ((to // 16) % 2 == (at // 32) % 2) & (to % 2 == (at // 64) % 2) & ((to // 2) % 2 == at // 128)
    value = jnp.zeros((256, 128), F32)
    for k in range(3):
        value = jnp.where(fits & ((to % 16) // 4 == k), by_map[:, k : k + 1], value)
    for block in range(4):
        wh[block * 256 : block * 256 + 256, :] = jnp.where(to // 32 == block, value, 0.0).astype(BF16)


def main_kernel(
    nb, depth, prev, own, nxt, recv, wf, ws, wc, wu, wh, out, ext, strips, turned, taps,
    edge_taps, first, edge_mean, pooled, skip, high, low, mixed
):

    strips[...] = jnp.zeros(strips.shape, F32)
    ext[...] = jnp.zeros(ext.shape, F32)
    edge_taps[...] = jnp.zeros(edge_taps.shape, F32)
    for k in range(8):
        have = nb[0, k] >= 0
        for step in range(3):
            near = depth[0, 0] + step - 1
            strip = recv[jnp.clip(near, 0, 3) * 32 + jnp.maximum(nb[0, k], 0)].astype(F32)
            strips[k, 4 + 8 * step : 12 + 8 * step, :] = jnp.where(have & (near >= 0) & (near < 4), strip, 0.0)
        strips[k, 28:32, :] = jnp.full((4, 128), jnp.where(have, 0.0, 1.0), F32)

    for z in range(7):
        if z < 6:
            plane = (prev, own, nxt)[z // 2][z % 2].astype(F32)
            there = (depth[0, 0] > 0, True, depth[0, 0] < 3)[z // 2]
            ext[z, 4:132, :] = jnp.where(there, plane, 0.0)
        ext[z, 0:4, :] = strips[0, 4 * z + 4 : 4 * z + 8, :]
        ext[z, 132:136, :] = strips[1, 4 * z + 4 : 4 * z + 8, :]

    lane = iota((8, 128), 1)
    def first_rows(base, count):
        window = jnp.concatenate([taps[pl.ds(base, count), :], taps[pl.ds(base + 32, count), :]], axis=1)
        for n in range(0, 2304, 256):
            first[pl.ds(base, count), n : n + 256] = jnp.maximum(dot(window, wf[:, n : n + 256]), 0.0).astype(BF16)

    done = 0
    for b in range(9):
        lines = [ext[z, 16 * b : 16 * b + 16, :] for z in range(8)]
        turned[b, 8:136, :] = jnp.concatenate(lines, axis=0).T
        for start, sides, shift in ((0, (4, 2, 6), 0), (136, (5, 3, 7), 4)):
            value = jnp.zeros((8, 128), F32)
            for z in range(7):
                rows = slice(4 * z + shift, 4 * z + shift + 8)
                line = strips[sides[1], rows, :]
                if b == 0:
                    line = jnp.where(lane >= 124, strips[sides[0], rows, :], line)
                if b == 8:
                    line = jnp.where(lane < 4, strips[sides[2], rows, :], jnp.where(lane >= 124, line, 0.0))
                turn = (16 * z - 16 * b + 4) % 128
                value = jnp.where(lane // 16 == z, pltpu.roll(line, turn, 1) if turn else line, value)
            turned[b, start : start + 8, :] = value
        parts = [
            jnp.concatenate(
                [turned[b, pl.ds(6 + c, 32, stride=4), :], turned[b, pl.ds(2 + c, 2, stride=132), :]], axis=0
            )
            for c in range(8)
        ]
        for bit in (1, 2, 4):
            side = (iota((34, 128), 1) // (2 * bit)) % 2 == 0
            for a in range(8):
                if not a & bit:
                    one, two = parts[a], parts[a + bit]
                    parts[a] = jnp.where(side, one, pltpu.roll(two, 2 * bit, 1))
                    parts[a + bit] = jnp.where(side, pltpu.roll(one, 128 - 2 * bit, 1), two)
        for y in range(8):
            at = 8 * b + y
            if at < 68:
                taps[at * 32 : at * 32 + 32, :] = parts[y][0:32].astype(BF16)
                edge_taps[0, at : at + 1, :] = parts[y][32:33]
                edge_taps[1, at : at + 1, :] = parts[y][33:34]
        if b in FIRST_AFTER:
            ready = min(8 * b + 7, 67)
            first_rows(done * 32, (ready - done) * 32)
            done = ready

    at, to = iota((256, 256), 0), iota((256, 256), 1)
    meets = (at // 128 == to // 128) & (at % 32 == to % 32)
    outside = ((depth[0, 0] == 0, False), (False, depth[0, 0] == 3))
    pools, scales = [], []
    for p in range(2):
        low_plane, high_plane = (jnp.where(gone, 0.0, 0.25) for gone in outside[p])
        scales.append((low_plane, high_plane))
        scale = jnp.where(to < 128, jnp.where(outside[p][0], 0.0, 0.25), jnp.where(outside[p][1], 0.0, 0.25))
        pools.append([jnp.where(meets & ((to // 32) % 2 != par), scale, 0.0).astype(BF16) for par in range(2)])

    def add_dots(pairs):
        total = None
        for a, b in pairs:
            term = dot(a, b)
            total = term if total is None else total + term
        return total

    windows = []
    for side in range(2):
        lines = [edge_taps[side, pl.ds(dy, 80), :].astype(BF16) for dy in range(3)]
        windows += [jnp.concatenate(lines[dy : dy + 2], axis=1) for dy in range(2)]
    edges = jnp.maximum(dot(jnp.concatenate(windows, axis=0), wf[...]), 0.0).astype(BF16)
    for p in range(2):
        pairs = []
        for z in range(4):
            for dy in range(2):
                lanes = (2 * p + z) * 384
                west = edges[dy * 80 : dy * 80 + 80, lanes + 128 : lanes + 384]
                east = edges[160 + dy * 80 : 240 + dy * 80, lanes : lanes + 256]
                pairs.append((jnp.concatenate([west, east], axis=0), ws[(z * 2 + dy) * 256 : (z * 2 + dy) * 256 + 256, :]))
        value = jnp.maximum(add_dots(pairs), 0.0).astype(BF16)
        edge_mean[p, 0] = dot(value[0:80], pools[p][1])
        edge_mean[p, 1] = dot(value[80:160], pools[p][0])

    group = iota((1, 128), 1) // 32
    tile_row, tile_group = iota((8, 256), 0), (iota((8, 256), 1) // 32) % 4
    at_west, at_east = (tile_row == 0) & (tile_group == 0), (tile_row == 7) & (tile_group == 3)

    def skip_rows(top, lines):
        base, count = top * 32, lines * 32
        for p in range(2):
            totals, values = [None, None], []
            for z in range(4):
                for dy in range(2):
                    at = (z * 2 + dy) * 256
                    for par in range(2):
                        lanes = (2 * p + z) * 384 + par * 128
                        term = dot(first[pl.ds(base + dy * 32, count), lanes : lanes + 256], ws[at : at + 256, :])
                        totals[par] = term if totals[par] is None else totals[par] + term
            for par in range(2):
                value = jnp.maximum(totals[par], 0.0).astype(BF16)
                skip[par, pl.ds(base, count), p * 128 : p * 128 + 128] = value[:, 128 - p * 128 : 256 - p * 128]
                values.append(value)
            halves = []
            for half in range(2):
                sums = []
                for value in values:
                    part = value[:, half * 128 : half * 128 + 128].astype(F32)
                    part = part + pltpu.roll(part, 32, 1)
                    sums.append(part + pltpu.roll(part, 64, 1))
                mean = jnp.where(group % 2 == 1, sums[0], sums[1]) * scales[p][half]
                before, after = pltpu.roll(mean, 1, 0), pltpu.roll(mean, count - 1, 0)
                halves.append(jnp.where(group == 0, before, jnp.where(group == 3, after, mean)))
            mean = jnp.concatenate(halves, axis=1)
            for y in range(lines):
                west = edge_mean[p, 0, top + y : top + y + 1, :]
                east = edge_mean[p, 1, top + y : top + y + 1, :]
                line = [mean[y * 32 + at : y * 32 + at + 8] for at in range(0, 32, 8)]
                line[0] = jnp.where(at_west, west, line[0])
                line[3] = jnp.where(at_east, east, line[3])
                pooled[p, pl.ds(base + y * 32, 32), :] = jnp.concatenate(line, axis=0).astype(BF16)

    top = 0
    for lines in SKIP_STEPS:
        skip_rows(top, lines)
        top += lines


    def last_rows(tops, lines):
        count = lines * 32
        totals = [None] * len(tops)
        for dy in range(3):
            for p in range(2):
                at = (dy * 2 + p) * 256
                for i, top in enumerate(tops):
                    term = dot(pooled[p, pl.ds(top * 32 + dy * 32, count), :], wc[at : at + 256, :])
                    totals[i] = term if totals[i] is None else totals[i] + term
        coarse = [jnp.maximum(total, 0.0).astype(BF16) for total in totals]
        joined = [[] for _ in tops]
        for side in range(2):
            for i, top in enumerate(tops):
                upward = dot(coarse[i][:, side * 128 : side * 128 + 128], wu[...])
                upward = upward + skip[side, pl.ds(top * 32 + 32, count), :].astype(F32)
                joined[i].append(jnp.maximum(upward, 0.0).astype(BF16))
        blocks = [
            [
                jnp.concatenate([part[side][at + half * 128 : at + half * 128 + 128] for at in range(0, count, 256)], axis=0)
                for side in range(2)
                for half in range(2)
            ]
            for part in joined
        ]
        mapped = [dot(jnp.concatenate(block, axis=1), wh[...]) for block in blocks]
        for i, top in enumerate(tops):
            for eight in range(lines // 8):
                logits = mapped[i][eight * 128 : eight * 128 + 128].T
                rounded = logits.astype(BF16)
                rest = (logits - rounded.astype(F32)).astype(BF16)
                for half in range(2):
                    rows = pl.ds(top * 4 + eight * 32 + half * 16, 16)
                    for side in range(2):
                        for px in range(2):
                            at = side * 64 + half * 32 + px * 16
                            lanes = slice((side * 2 + px) * 128, (side * 2 + px) * 128 + 128)
                            high[rows, lanes] = rounded[at : at + 16]
                            low[rows, lanes] = rest[at : at + 16]

    for tops, lines in LAST_STEPS:
        last_rows(tops, lines)

    at, to = iota((128, 512), 0), iota((128, 512), 1)
    same_line = at // 32 == to // 128
    offset = to % 128 - 4 * (at % 32)
    place = jnp.concatenate(
        [jnp.where(same_line & (offset == part), 1.0, 0.0).astype(BF16) for part in range(4)], axis=0
    )
    logits = dot(high[...], place) + dot(low[...], place)
    for line in range(4):
        mixed[line] = logits[:, line * 128 : line * 128 + 128]
    for k in range(3):
        for z in range(2):
            for py in range(2):
                for line in range(4):
                    row = k * 4 + z * 2 + py
                    out[0, k, z, pl.ds(2 * line + py, 16, stride=8), :] = mixed[line, pl.ds(row, 16, stride=16), :]


def on_device(em_volume, neighbours, first_kernel, second_kernel, coarse_kernel, up_kernel, head_kernel):
    own = em_volume[0]
    steps = lax.axis_size("gz")
    place = jnp.full((1, 1), lax.axis_index("gz"), jnp.int32)
    limit = pltpu.CompilerParams(vmem_limit_bytes=56 * 2**20)
    image = jax.ShapeDtypeStruct(own.shape, BF16)

    slots, sent = pl.pallas_call(
        pack_kernel,
        out_shape=[jax.ShapeDtypeStruct((128, 8, 128), BF16), image],
        in_specs=[SMEM, SMEM, VMEM],
        out_specs=[VMEM, VMEM],
        scratch_shapes=[pltpu.VMEM((4, 8, 128), F32)],
        compiler_params=limit,
        name="pack",
    )(neighbours, place, own)
    recv = lax.all_to_all(slots, ("gz", "xy"), 0, 0, tiled=True)
    prev = lax.ppermute(sent, "gz", [(i, (i + 1) % steps) for i in range(steps)])
    nxt = lax.ppermute(sent, "gz", [((i + 1) % steps, i) for i in range(steps)])

    shapes = [(256, 2304), (2048, 256), (1536, 256), (128, 256), (1024, 128)]
    weights = pl.pallas_call(
        weights_kernel,
        out_shape=[jax.ShapeDtypeStruct(s, BF16) for s in shapes],
        in_specs=[VMEM] * 6,
        out_specs=[VMEM] * 5,
        scratch_shapes=[
            pltpu.VMEM((896, 128), F32),
            pltpu.VMEM((864, 128), F32),
            pltpu.VMEM((128, 128), F32),
            pltpu.VMEM((28, 8, 128), F32),
        ],
        compiler_params=limit,
        cost_estimate=pl.CostEstimate(flops=10**8, bytes_accessed=4 * 10**6, transcendentals=0),
        name="weights",
    )(
        sent,
        first_kernel.T,
        jnp.transpose(second_kernel, (2, 0, 1)),
        jnp.transpose(coarse_kernel, (2, 1, 0)),
        jnp.transpose(up_kernel, (0, 2, 1)),
        head_kernel,
    )

    return pl.pallas_call(
        main_kernel,
        out_shape=jax.ShapeDtypeStruct((1, 3, 2, 128, 128), F32),
        in_specs=[SMEM] * 2 + [VMEM] * 9,
        out_specs=VMEM,
        scratch_shapes=[
            pltpu.VMEM((8, 144, 128), F32),
            pltpu.VMEM((8, 40, 128), F32),
            pltpu.VMEM((9, 144, 128), F32),
            pltpu.VMEM((68 * 32, 128), BF16),
            pltpu.VMEM((2, 88, 128), F32),
            pltpu.VMEM((67 * 32, 2304), BF16),
            pltpu.VMEM((2, 2, 80, 256), F32),
            pltpu.VMEM((2, LINES * 32, 256), BF16),
            pltpu.VMEM((2, LINES * 32, 256), BF16),
            pltpu.VMEM((256, 512), BF16),
            pltpu.VMEM((256, 512), BF16),
            pltpu.VMEM((4, 256, 128), F32),
        ],
        compiler_params=limit,
        name="layers",
    )(neighbours, place, prev, own, nxt, recv, *weights)


def solution(mesh):
    placed = (P("xy", "gz", None, None), P("xy", None), P(), P(), P(), P(), P())
    return jax.shard_map(
        on_device,
        mesh=mesh,
        in_specs=placed,
        out_specs=P("xy", None, "gz", None, None),
        check_vma=False,
    )
```

```python
import jax
import jax.numpy as jnp
from jax import lax
from jax.experimental import pallas as pl
from jax.experimental.pallas import tpu as pltpu
from jax.sharding import PartitionSpec as P

F32 = jnp.float32
BF16 = jnp.bfloat16
LINES = 66
FIRST_AFTER = (1, 3, 5, 8)
SKIP_STEPS = (11,) * 6
LAST_STEPS = (((0, 16), 16), ((32, 48), 16))
FIRST_OFF = 256.0
SKIP_OFF = 65536.0
VMEM = pl.BlockSpec(memory_space=pltpu.VMEM)
SMEM = pl.BlockSpec(memory_space=pltpu.SMEM)
NT = (((1,), (1,)), ((), ()))


def iota(shape, dim):
    return lax.broadcasted_iota(jnp.int32, shape, dim)


def dot(a, b):
    return jnp.dot(a, b, preferred_element_type=F32)


def dot_nt(a, b):
    return lax.dot_general(a, b, NT, preferred_element_type=F32)


def pack_kernel(nb, place, own, slots, sent, rows):
    sent[...] = own[...]
    lane, line = iota((16, 128), 1), iota((16, 128), 0)
    edge = jnp.where((lane == jnp.where(line < 4, line, 120 + line)) & (line < 8), 1.0, 0.0).astype(BF16)
    planes = jnp.concatenate([own[0], own[1]], axis=0)
    sides = dot_nt(edge, planes)
    for z in range(2):
        at = slice(4 * z, 4 * z + 4)
        rows[0, at, :] = planes[z * 128 : z * 128 + 16].astype(F32)[0:4]
        rows[1, at, :] = planes[z * 128 + 112 : z * 128 + 128].astype(F32)[12:16]
        rows[2, at, :] = sides[0:4, z * 128 : z * 128 + 128]
        rows[3, at, :] = sides[4:8, z * 128 : z * 128 + 128]
    for step in (-1, 0, 1):
        depth = place[0, 0] + step
        for k, strip in enumerate((0, 1, 2, 3, 2, 3, 2, 3)):

            @pl.when((nb[0, k] >= 0) & (depth >= 0) & (depth < 4))
            def _():
                slots[jnp.clip(depth, 0, 3) * 32 + jnp.maximum(nb[0, k], 0)] = rows[strip].astype(BF16)


def weights_kernel(own, first, second, coarse, up, head, wf, ws, wc, wu, wh, taps2, tapsc, part, ups):
    lane = iota((32, 128), 1)
    part[...] = jnp.zeros(part.shape, F32)
    for four in range(7):
        value = jnp.zeros((32, 128), F32)
        for tap in range(4 * four, min(4 * four + 4, 27)):
            part[0:28, 0:28] = second[tap].astype(F32)
            turn = (tap % 4) * 32
            value = value + (pltpu.roll(part[0:32, :], turn, 1) if turn else part[0:32, :])
        turned = jnp.concatenate([value] * 4, axis=0).T
        taps2[four * 128 : four * 128 + 128, :] = turned
    fill = jnp.where(iota((1, 128), 1) % 32 < 28, -SKIP_OFF, 0.0)
    taps2[13 * 32 + 28 : 13 * 32 + 29, :] = fill
    for z in range(4):
        for row in range(4):
            for col in range(4):
                block = (z * 2 + row // 2) * 8 + (col // 2) * 4 + (row % 2) * 2 + col % 2
                for half in range(2):
                    value = jnp.zeros((32, 128), F32)
                    for slot in range(4):
                        dz, dr, dc = z - half, row - slot // 2, col - slot % 2
                        if 0 <= dz < 3 and 0 <= dr < 3 and 0 <= dc < 3:
                            tap = dz * 9 + dr * 3 + dc
                            value = jnp.where(lane // 32 == slot, taps2[tap * 32 : tap * 32 + 32, :], value)
                    ws[block * 32 : block * 32 + 32, half * 128 : half * 128 + 128] = value.astype(BF16)
    part[...] = jnp.zeros(part.shape, F32)
    for tap in range(27):
        part[0:28, 0:56] = coarse[tap].astype(F32)
        tapsc[tap * 32 : tap * 32 + 32, :] = part[0:32, :] + pltpu.roll(part[0:32, :], 64, 1)
    for dy in range(3):
        for z in range(4):
            for col in range(4):
                block = (dy * 4 + z) * 4 + col
                for half in range(2):
                    value = jnp.zeros((32, 128), F32)
                    for slot in range(2):
                        dz, dc = z - slot, col - half
                        if 0 <= dz < 3 and 0 <= dc < 3:
                            tap = dz * 9 + dy * 3 + dc
                            value = jnp.where(lane // 64 == slot, tapsc[tap * 32 : tap * 32 + 32, :], value)
                    wc[block * 32 : block * 32 + 32, half * 128 : half * 128 + 128] = value.astype(BF16)
    part[...] = jnp.zeros(part.shape, F32)
    ups[...] = jnp.zeros(ups.shape, F32)
    ups[:, 0:4, 0:56] = up[...].astype(F32)
    for channel in range(28):
        part[pl.ds(channel, 4, stride=32), :] = ups[channel, 0:4, :]
    mixed = part[...].T[0:64].astype(BF16)
    nothing = jnp.zeros((64, 128), BF16)
    wu[0:64, 0:128] = mixed
    wu[0:64, 128:256] = nothing
    wu[64:128, 0:128] = nothing
    wu[64:128, 128:256] = mixed
    part[...] = jnp.zeros(part.shape, F32)
    part[0:9, 0:28] = first[...].astype(F32)
    by_tap = part[0:16, :]
    by_tap = by_tap + pltpu.roll(by_tap, 32, 1)
    by_tap = by_tap + pltpu.roll(by_tap, 64, 1)
    by_tap = jnp.concatenate([by_tap] * 3, axis=1)
    at, to = iota((256, 384), 0), iota((256, 384), 1)
    row = (at // 128) * 2 + at % 2 - (to // 64) % 2
    col = (at // 2) % 8 - (to // 128) * 2 - (to // 32) % 2
    plane = (at // 16) % 8
    window = jnp.where((row >= 0) & (row < 3) & (col >= 0) & (col < 3), row * 3 + col, -1)
    spread = jnp.zeros((256, 384), F32)
    for tap in range(9):
        spread = jnp.where(window == tap, by_tap[tap : tap + 1, :], spread)
    off = jnp.where(to % 32 < 28, -FIRST_OFF, jnp.where(to % 32 == 28, 1.0, 0.0))
    off = jnp.where((window == 4) & (plane == 6), off, 0.0)
    for z in range(6):
        wf[:, z * 384 : z * 384 + 384] = jnp.where(plane == z, spread, off).astype(BF16)
    part[...] = jnp.zeros(part.shape, F32)
    part[0:3, 0:28] = head[...].astype(F32)
    by_map = part[...].T
    by_map = jnp.concatenate([by_map[0:32]] * 8, axis=0)
    at, to = iota((256, 128), 0), iota((256, 128), 1)
    fits = ((to // 16) % 2 == (at // 32) % 2) & (to % 2 == (at // 64) % 2) & ((to // 2) % 2 == at // 128)
    value = jnp.zeros((256, 128), F32)
    for k in range(3):
        value = jnp.where(fits & ((to % 16) // 4 == k), by_map[:, k : k + 1], value)
    for block in range(4):
        wh[block * 256 : block * 256 + 256, :] = jnp.where(to // 32 == block, value, 0.0).astype(BF16)


def main_kernel(
    nb, depth, prev, own, nxt, recv, wf, ws, wc, wu, wh, out, ext, strips, turned, taps,
    edge_taps, first, edge_mean, pooled, skip, high, low, mixed
):

    strips[...] = jnp.zeros(strips.shape, F32)
    ext[...] = jnp.zeros(ext.shape, F32)
    edge_taps[...] = jnp.zeros(edge_taps.shape, F32)
    for k in range(8):
        have = nb[0, k] >= 0
        for step in range(3):
            near = depth[0, 0] + step - 1
            strip = recv[jnp.clip(near, 0, 3) * 32 + jnp.maximum(nb[0, k], 0)].astype(F32)
            strips[k, 4 + 8 * step : 12 + 8 * step, :] = jnp.where(have & (near >= 0) & (near < 4), strip, 0.0)
        strips[k, 28:32, :] = jnp.full((4, 128), jnp.where(have, 0.0, 1.0), F32)

    for z in range(7):
        if z < 6:
            plane = (prev, own, nxt)[z // 2][z % 2].astype(F32)
            there = (depth[0, 0] > 0, True, depth[0, 0] < 3)[z // 2]
            ext[z, 4:132, :] = jnp.where(there, plane, 0.0)
        ext[z, 0:4, :] = strips[0, 4 * z + 4 : 4 * z + 8, :]
        ext[z, 132:136, :] = strips[1, 4 * z + 4 : 4 * z + 8, :]

    lane = iota((8, 128), 1)
    def first_rows(base, count):
        window = jnp.concatenate([taps[pl.ds(base, count), :], taps[pl.ds(base + 32, count), :]], axis=1)
        for n in range(0, 2304, 256):
            first[pl.ds(base, count), n : n + 256] = jnp.maximum(dot(window, wf[:, n : n + 256]), 0.0).astype(BF16)

    done = 0
    for b in range(9):
        lines = [ext[z, 16 * b : 16 * b + 16, :] for z in range(8)]
        turned[b, 8:136, :] = jnp.concatenate(lines, axis=0).T
        for start, sides, shift in ((0, (4, 2, 6), 0), (136, (5, 3, 7), 4)):
            value = jnp.zeros((8, 128), F32)
            for z in range(7):
                rows = slice(4 * z + shift, 4 * z + shift + 8)
                line = strips[sides[1], rows, :]
                if b == 0:
                    line = jnp.where(lane >= 124, strips[sides[0], rows, :], line)
                if b == 8:
                    line = jnp.where(lane < 4, strips[sides[2], rows, :], jnp.where(lane >= 124, line, 0.0))
                turn = (16 * z - 16 * b + 4) % 128
                value = jnp.where(lane // 16 == z, pltpu.roll(line, turn, 1) if turn else line, value)
            turned[b, start : start + 8, :] = value
        parts = [
            jnp.concatenate(
                [turned[b, pl.ds(6 + c, 32, stride=4), :], turned[b, pl.ds(2 + c, 2, stride=132), :]], axis=0
            )
            for c in range(8)
        ]
        for bit in (1, 2, 4):
            side = (iota((34, 128), 1) // (2 * bit)) % 2 == 0
            for a in range(8):
                if not a & bit:
                    one, two = parts[a], parts[a + bit]
                    parts[a] = jnp.where(side, one, pltpu.roll(two, 2 * bit, 1))
                    parts[a + bit] = jnp.where(side, pltpu.roll(one, 128 - 2 * bit, 1), two)
        for y in range(8):
            at = 8 * b + y
            if at < 68:
                taps[at * 32 : at * 32 + 32, :] = parts[y][0:32].astype(BF16)
                edge_taps[0, at : at + 1, :] = parts[y][32:33]
                edge_taps[1, at : at + 1, :] = parts[y][33:34]
        if b in FIRST_AFTER:
            ready = min(8 * b + 7, 67)
            first_rows(done * 32, (ready - done) * 32)
            done = ready

    at, to = iota((256, 256), 0), iota((256, 256), 1)
    meets = (at // 128 == to // 128) & (at % 32 == to % 32)
    outside = ((depth[0, 0] == 0, False), (False, depth[0, 0] == 3))
    pools, scales = [], []
    for p in range(2):
        low_plane, high_plane = (jnp.where(gone, 0.0, 0.25) for gone in outside[p])
        scales.append((low_plane, high_plane))
        scale = jnp.where(to < 128, jnp.where(outside[p][0], 0.0, 0.25), jnp.where(outside[p][1], 0.0, 0.25))
        pools.append([jnp.where(meets & ((to // 32) % 2 != par), scale, 0.0).astype(BF16) for par in range(2)])

    def add_dots(pairs):
        total = None
        for a, b in pairs:
            term = dot(a, b)
            total = term if total is None else total + term
        return total

    windows = []
    for side in range(2):
        lines = [edge_taps[side, pl.ds(dy, 80), :].astype(BF16) for dy in range(3)]
        windows += [jnp.concatenate(lines[dy : dy + 2], axis=1) for dy in range(2)]
    edges = jnp.maximum(dot(jnp.concatenate(windows, axis=0), wf[...]), 0.0).astype(BF16)
    totals = [None, None]
    for z in range(4):
        for dy in range(2):
            at = (z * 2 + dy) * 256
            for p in range(2):
                lanes = (2 * p + z) * 384
                west = edges[dy * 80 : dy * 80 + 80, lanes + 128 : lanes + 384]
                east = edges[160 + dy * 80 : 240 + dy * 80, lanes : lanes + 256]
                term = dot(jnp.concatenate([west, east], axis=0), ws[at : at + 256, :])
                totals[p] = term if totals[p] is None else totals[p] + term
    for p in range(2):
        value = jnp.maximum(totals[p], 0.0).astype(BF16)
        edge_mean[p, 0] = dot(value[0:80], pools[p][1])
        edge_mean[p, 1] = dot(value[80:160], pools[p][0])

    group = iota((1, 128), 1) // 32
    tile_row, tile_group = iota((8, 256), 0), (iota((8, 256), 1) // 32) % 4
    at_west, at_east = (tile_row == 0) & (tile_group == 0), (tile_row == 7) & (tile_group == 3)

    def skip_rows(top, lines):
        base, count = top * 32, lines * 32
        for p in range(2):
            totals, values = [None, None], []
            for z in range(4):
                for dy in range(2):
                    at = (z * 2 + dy) * 256
                    for par in range(2):
                        lanes = (2 * p + z) * 384 + par * 128
                        term = dot(first[pl.ds(base + dy * 32, count), lanes : lanes + 256], ws[at : at + 256, :])
                        totals[par] = term if totals[par] is None else totals[par] + term
            for par in range(2):
                value = jnp.maximum(totals[par], 0.0).astype(BF16)
                skip[par, pl.ds(base, count), p * 128 : p * 128 + 128] = value[:, 128 - p * 128 : 256 - p * 128]
                values.append(value)
            halves = []
            for half in range(2):
                sums = []
                for value in values:
                    part = value[:, half * 128 : half * 128 + 128].astype(F32)
                    part = part + pltpu.roll(part, 32, 1)
                    sums.append(part + pltpu.roll(part, 64, 1))
                mean = jnp.where(group % 2 == 1, sums[0], sums[1]) * scales[p][half]
                before, after = pltpu.roll(mean, 1, 0), pltpu.roll(mean, count - 1, 0)
                halves.append(jnp.where(group == 0, before, jnp.where(group == 3, after, mean)))
            mean = jnp.concatenate(halves, axis=1)
            for y in range(lines):
                west = edge_mean[p, 0, top + y : top + y + 1, :]
                east = edge_mean[p, 1, top + y : top + y + 1, :]
                line = [mean[y * 32 + at : y * 32 + at + 8] for at in range(0, 32, 8)]
                line[0] = jnp.where(at_west, west, line[0])
                line[3] = jnp.where(at_east, east, line[3])
                pooled[p, pl.ds(base + y * 32, 32), :] = jnp.concatenate(line, axis=0).astype(BF16)

    top = 0
    for lines in SKIP_STEPS:
        skip_rows(top, lines)
        top += lines


    def last_rows(tops, lines):
        count = lines * 32
        totals = [None] * len(tops)
        for dy in range(3):
            for p in range(2):
                at = (dy * 2 + p) * 256
                for i, top in enumerate(tops):
                    term = dot(pooled[p, pl.ds(top * 32 + dy * 32, count), :], wc[at : at + 256, :])
                    totals[i] = term if totals[i] is None else totals[i] + term
        coarse = [jnp.maximum(total, 0.0).astype(BF16) for total in totals]
        joined = [[] for _ in tops]
        for side in range(2):
            for i, top in enumerate(tops):
                upward = dot(coarse[i][:, side * 128 : side * 128 + 128], wu[...])
                upward = upward + skip[side, pl.ds(top * 32 + 32, count), :].astype(F32)
                joined[i].append(jnp.maximum(upward, 0.0).astype(BF16))
        blocks = [
            [
                jnp.concatenate([part[side][at + half * 128 : at + half * 128 + 128] for at in range(0, count, 256)], axis=0)
                for side in range(2)
                for half in range(2)
            ]
            for part in joined
        ]
        mapped = [dot(jnp.concatenate(block, axis=1), wh[...]) for block in blocks]
        for i, top in enumerate(tops):
            for eight in range(lines // 8):
                logits = mapped[i][eight * 128 : eight * 128 + 128].T
                rounded = logits.astype(BF16)
                rest = (logits - rounded.astype(F32)).astype(BF16)
                for half in range(2):
                    rows = pl.ds(top * 4 + eight * 32 + half * 16, 16)
                    for side in range(2):
                        for px in range(2):
                            at = side * 64 + half * 32 + px * 16
                            lanes = slice((side * 2 + px) * 128, (side * 2 + px) * 128 + 128)
                            high[rows, lanes] = rounded[at : at + 16]
                            low[rows, lanes] = rest[at : at + 16]

    for tops, lines in LAST_STEPS:
        last_rows(tops, lines)

    at, to = iota((128, 512), 0), iota((128, 512), 1)
    same_line = at // 32 == to // 128
    offset = to % 128 - 4 * (at % 32)
    place = jnp.concatenate(
        [jnp.where(same_line & (offset == part), 1.0, 0.0).astype(BF16) for part in range(4)], axis=0
    )
    logits = dot(high[...], place) + dot(low[...], place)
    for line in range(4):
        mixed[line] = logits[:, line * 128 : line * 128 + 128]
    for k in range(3):
        for z in range(2):
            for py in range(2):
                for line in range(4):
                    row = k * 4 + z * 2 + py
                    out[0, k, z, pl.ds(2 * line + py, 16, stride=8), :] = mixed[line, pl.ds(row, 16, stride=16), :]


def on_device(em_volume, neighbours, first_kernel, second_kernel, coarse_kernel, up_kernel, head_kernel):
    own = em_volume[0]
    steps = lax.axis_size("gz")
    place = jnp.full((1, 1), lax.axis_index("gz"), jnp.int32)
    limit = pltpu.CompilerParams(vmem_limit_bytes=56 * 2**20)
    image = jax.ShapeDtypeStruct(own.shape, BF16)

    slots, sent = pl.pallas_call(
        pack_kernel,
        out_shape=[jax.ShapeDtypeStruct((128, 8, 128), BF16), image],
        in_specs=[SMEM, SMEM, VMEM],
        out_specs=[VMEM, VMEM],
        scratch_shapes=[pltpu.VMEM((4, 8, 128), F32)],
        compiler_params=limit,
        name="pack",
    )(neighbours, place, own)
    recv = lax.all_to_all(slots, ("gz", "xy"), 0, 0, tiled=True)
    prev = lax.ppermute(sent, "gz", [(i, (i + 1) % steps) for i in range(steps)])
    nxt = lax.ppermute(sent, "gz", [((i + 1) % steps, i) for i in range(steps)])

    shapes = [(256, 2304), (2048, 256), (1536, 256), (128, 256), (1024, 128)]
    weights = pl.pallas_call(
        weights_kernel,
        out_shape=[jax.ShapeDtypeStruct(s, BF16) for s in shapes],
        in_specs=[VMEM] * 6,
        out_specs=[VMEM] * 5,
        scratch_shapes=[
            pltpu.VMEM((896, 128), F32),
            pltpu.VMEM((864, 128), F32),
            pltpu.VMEM((128, 128), F32),
            pltpu.VMEM((28, 8, 128), F32),
        ],
        compiler_params=limit,
        cost_estimate=pl.CostEstimate(flops=10**8, bytes_accessed=4 * 10**6, transcendentals=0),
        name="weights",
    )(
        sent,
        first_kernel.T,
        jnp.transpose(second_kernel, (2, 0, 1)),
        jnp.transpose(coarse_kernel, (2, 1, 0)),
        jnp.transpose(up_kernel, (0, 2, 1)),
        head_kernel,
    )

    return pl.pallas_call(
        main_kernel,
        out_shape=jax.ShapeDtypeStruct((1, 3, 2, 128, 128), F32),
        in_specs=[SMEM] * 2 + [VMEM] * 9,
        out_specs=VMEM,
        scratch_shapes=[
            pltpu.VMEM((8, 144, 128), F32),
            pltpu.VMEM((8, 40, 128), F32),
            pltpu.VMEM((9, 144, 128), F32),
            pltpu.VMEM((68 * 32, 128), BF16),
            pltpu.VMEM((2, 88, 128), F32),
            pltpu.VMEM((67 * 32, 2304), BF16),
            pltpu.VMEM((2, 2, 80, 256), F32),
            pltpu.VMEM((2, LINES * 32, 256), BF16),
            pltpu.VMEM((2, LINES * 32, 256), BF16),
            pltpu.VMEM((256, 512), BF16),
            pltpu.VMEM((256, 512), BF16),
            pltpu.VMEM((4, 256, 128), F32),
        ],
        compiler_params=limit,
        name="layers",
    )(neighbours, place, prev, own, nxt, recv, *weights)


def solution(mesh):
    placed = (P("xy", "gz", None, None), P("xy", None), P(), P(), P(), P(), P())
    return jax.shard_map(
        on_device,
        mesh=mesh,
        in_specs=placed,
        out_specs=P("xy", None, "gz", None, None),
        check_vma=False,
    )
```
